32 devices in a mesh: groups: 2 (over y), seq: 4 (over z), tensor: 4 (over x, core).
Axes of the slice: x: 2, y: 2, z: 4, core: 2. Of those that a mesh axis runs over, the one named last changes fastest.
Arguments:
- residual_in: float32 [1024, 4096], P(('groups', 'seq'), 'tensor'), parts along dimension 0, may hold values from -48 to 48
- norm_gain: float32 [4096], replicated, may hold values from 0.1 to 1.9
- in_weight: bfloat16 [3, 4096, 2048], P(None, 'seq', 'tensor'), may hold values from -0.09375 to 0.09375
- short_taps: float32 [3, 3, 2048], P(None, None, 'tensor'), may hold values from -3 to 3
- long_filter: float32 [2048, 512], P(('tensor', 'seq')), may hold values from -0.25 to 0.25
- out_weight: bfloat16 [4096, 2048], P('seq', 'tensor'), may hold values from -0.125 to 0.125
Outputs:
- block_out: float32 [1024, 4096], P(('groups', 'seq'), 'tensor'), parts along dimension 0
The draws below stay inside these ranges and needn't reach their ends.
There are 2 independent parts, one for each index of `groups`. The reference program is written for one: setup_inputs(seed, part) draws one part's arguments, and reference() takes and returns one part's arrays. A program takes and returns all parts, laid end to end along the dimension named above; an argument that names none is the same for every part. Nothing has to cross between parts.
All inputs are finite; a program needn't handle non-finite values.
Results may differ from the reference program's by a relative error of at most 0.015.
Values may be sent and summed in bfloat16 or wider, within the bound.
A program may use at most 64 MiB of HBM per device.

```python
import math
import jax
import jax.numpy as jnp
from jax import lax

D = 4096
CH = 2048
TAPS = 3
L = 512
N_TENSOR = 4


def draw_residual_in(key, part):
    first, second, third = jax.random.split(key, 3)
    position = jnp.arange(D, dtype=jnp.float32) / D
    column_scale = 0.4 * jnp.exp(position * math.log(3.0)) * jnp.exp(jax.random.uniform(second, (D,), jnp.float32, 0.0, math.log(3.3)))
    row_scale = jnp.exp(jax.random.uniform(third, (L, 1), jnp.float32, math.log(0.3), math.log(3.0)))
    base = jax.random.truncated_normal(first, -4.0, 4.0, (L, D), jnp.float32)
    return base * row_scale * column_scale[None, :]


def level_of(rng, dims, cuts, least, largest):
    gain = 1.0
    for dim, shards_of in cuts:
        steps = jax.random.uniform(jax.random.fold_in(jax.random.fold_in(rng, 6), dim), (shards_of,), jnp.float32, least / len(cuts), largest / len(cuts))
        gain = gain * jnp.repeat(jnp.exp(steps), dims[dim] // shards_of).reshape((-1,) + (1,) * (len(dims) - 1 - dim))
    return gain


def normal_values(stream_key, extent, width, bound, shards=(), held_as=jnp.bfloat16):
    gain = level_of(stream_key, extent, shards, -0.22, 0.18) if shards else 1.0
    entries = jax.random.normal(stream_key, extent, jnp.float32) * width * gain
    return jnp.minimum(jnp.maximum(entries, -bound), bound).astype(held_as)


def setup_inputs(seed: int = 0, part: int = 0) -> dict:
    keys = jax.random.split(jax.random.key(seed), 7)
    part_splits = jax.random.split(jax.random.fold_in(keys[6], part), 7)
    residual_in = draw_residual_in(jax.random.fold_in(jax.random.fold_in(keys[6], part), 71), part)
    norm_gain = jnp.clip(1.0 + 0.18 * jax.random.normal(keys[1], (D,), jnp.float32), 0.1, 1.9)
    in_weight = normal_values(keys[2], (3, D, CH), D ** -0.5, 0.09375, ((1, 4), (2, 4)))
    short_taps = normal_values(keys[3], (3, TAPS, CH), 0.6, 3.0, ((2, 4),), jnp.float32)
    long_filter = normal_values(keys[4], (CH, L), L ** -0.5, 0.25, ((0, 16),), jnp.float32)
    out_weight = normal_values(keys[5], (D, CH), CH ** -0.5, 0.125, ((0, 4), (1, 4)))
    return {"residual_in": residual_in, "norm_gain": norm_gain, "in_weight": in_weight, "short_taps": short_taps, "long_filter": long_filter, "out_weight": out_weight}


def reference(residual_in, norm_gain, in_weight, short_taps, long_filter, out_weight):
    mean_sq = lax.optimization_barrier(jnp.mean(residual_in * residual_in, axis=1, keepdims=True))
    normed = (residual_in * lax.rsqrt(mean_sq + 1e-05) * norm_gain).astype(jnp.bfloat16)
    projected = jnp.einsum('ld,sdc->scl', normed.astype(jnp.float32), in_weight.astype(jnp.float32), precision=lax.Precision.HIGHEST)
    reach = TAPS - 1
    padded = jnp.pad(projected, ((0, 0), (0, 0), (reach, 0)))
    mixed = short_taps[:, 0, :, None] * projected
    for offset in range(1, TAPS):
        mixed = mixed + short_taps[:, offset, :, None] * padded[:, :, reach - offset:reach - offset + L]
    query = mixed[0]
    product_kv = mixed[1] * mixed[2]
    spectrum = jnp.fft.rfft(product_kv, n=2 * L, axis=1) * jnp.fft.rfft(long_filter, n=2 * L, axis=1)
    conv = jnp.fft.irfft(spectrum, n=2 * L, axis=1)[:, :L].astype(jnp.float32)
    gated = (query * conv).astype(jnp.bfloat16)
    block_width = CH // N_TENSOR
    summed = jnp.zeros((L, D), jnp.float32)
    for block in range(N_TENSOR):
        part_gated = gated[block * block_width:(block + 1) * block_width].astype(jnp.float32)
        part_weight = out_weight[:, block * block_width:(block + 1) * block_width].astype(jnp.float32)
        term = jnp.einsum('cl,dc->ld', part_gated, part_weight, precision=lax.Precision.HIGHEST)
        rounded = lax.optimization_barrier(term.astype(jnp.bfloat16))
        summed = summed + rounded.astype(jnp.float32)
    return residual_in + summed
```

```python
import math

import jax
import jax.numpy as jnp
from jax import lax
from jax.sharding import PartitionSpec as P

EPSILON = 1e-05


def shifted(value, axis, by):
    length = lax.axis_size(axis)
    pairs = [(i, i + by) for i in range(length) if 0 <= i + by < length]
    return lax.ppermute(value, axis, pairs)


def exact_product(form, left, right):
    return jnp.einsum(form, left, right, precision=lax.Precision.HIGHEST)


def angle_tables(modulus, count_a, count_b):
    index_a = jnp.arange(count_a, dtype=jnp.int32)[:, None]
    index_b = jnp.arange(count_b, dtype=jnp.int32)[None, :]
    theta = (index_a * index_b % modulus).astype(jnp.float32) * (2.0 * math.pi / modulus)
    return (jnp.cos(theta), jnp.sin(theta))


def split_length(full_length):
    low_factor = 1
    while full_length % (4 * low_factor) == 0 and 4 * low_factor * low_factor <= full_length:
        low_factor = low_factor * 2
    return (low_factor, full_length // low_factor)


def forward_spectrum(signal, low_factor, high_factor, all_tables):
    cos_high, sin_high, cos_twist, sin_twist, cos_low, sin_low = all_tables
    channel_count = signal.shape[0]
    blocks = signal.reshape(channel_count, high_factor // 2, low_factor)
    real_a = exact_product("cmp,mk->cpk", blocks, cos_high)
    imag_a = -exact_product("cmp,mk->cpk", blocks, sin_high)
    real_b = real_a * cos_twist + imag_a * sin_twist
    imag_b = imag_a * cos_twist - real_a * sin_twist
    real_x = exact_product("cpk,pj->cjk", real_b, cos_low) + exact_product(
        "cpk,pj->cjk", imag_b, sin_low
    )
    imag_x = exact_product("cpk,pj->cjk", imag_b, cos_low) - exact_product(
        "cpk,pj->cjk", real_b, sin_low
    )
    return (real_x, imag_x)


def inverse_signal(real_x, imag_x, low_factor, high_factor, all_tables):
    cos_high, sin_high, cos_twist, sin_twist, cos_low, sin_low = all_tables
    channel_count = real_x.shape[0]
    real_b = exact_product("cjk,pj->cpk", real_x, cos_low) - exact_product(
        "cjk,pj->cpk", imag_x, sin_low
    )
    imag_b = exact_product("cjk,pj->cpk", real_x, sin_low) + exact_product(
        "cjk,pj->cpk", imag_x, cos_low
    )
    real_c = real_b * cos_twist - imag_b * sin_twist
    imag_c = real_b * sin_twist + imag_b * cos_twist
    result = exact_product("cpk,mk->cmp", real_c, cos_high) - exact_product(
        "cpk,mk->cmp", imag_c, sin_high
    )
    full_length = low_factor * high_factor
    return (result / full_length).reshape(channel_count, full_length // 2)


def shards(residual_in, norm_gain, in_weight, short_taps, long_filter, out_weight):
    row_count, local_width = residual_in.shape
    full_rows = lax.all_gather(
        residual_in.astype(jnp.bfloat16), "tensor", axis=1, tiled=True
    ).astype(residual_in.dtype)
    mean_sq = jnp.mean(full_rows * full_rows, axis=1, keepdims=True)
    normed = (full_rows * lax.rsqrt(mean_sq + EPSILON) * norm_gain).astype(jnp.bfloat16)
    projected = jnp.einsum(
        "rd,sdc->scr",
        normed,
        lax.all_gather(in_weight, "seq", axis=1, tiled=True),
        preferred_element_type=jnp.float32,
    )
    reach = short_taps.shape[1] - 1
    earlier = shifted(projected[:, :, row_count - reach :], "seq", 1)
    extended = jnp.concatenate([earlier, projected], axis=2)
    mixed = short_taps[:, 0, :, None] * projected
    for offset in range(1, reach + 1):
        mixed = (
            mixed
            + short_taps[:, offset, :, None]
            * extended[:, :, reach - offset : reach - offset + row_count]
        )
    query = mixed[0]
    product_kv = mixed[1] * mixed[2]
    by_channel = lax.all_to_all(
        product_kv.astype(jnp.bfloat16), "seq", split_axis=0, concat_axis=1, tiled=True
    ).astype(product_kv.dtype)
    full_length = 2 * by_channel.shape[1]
    low_factor, high_factor = split_length(full_length)
    cos_high, sin_high = angle_tables(high_factor, high_factor // 2, high_factor)
    cos_twist, sin_twist = angle_tables(full_length, low_factor, high_factor)
    cos_low, sin_low = angle_tables(low_factor, low_factor, low_factor)
    all_tables = (cos_high, sin_high, cos_twist, sin_twist, cos_low, sin_low)
    signal_real, signal_imag = forward_spectrum(by_channel, low_factor, high_factor, all_tables)
    filter_real, filter_imag = forward_spectrum(long_filter, low_factor, high_factor, all_tables)
    conv = inverse_signal(
        signal_real * filter_real - signal_imag * filter_imag,
        signal_real * filter_imag + signal_imag * filter_real,
        low_factor,
        high_factor,
        all_tables,
    )
    returned = lax.all_to_all(
        conv.astype(jnp.bfloat16), "seq", split_axis=1, concat_axis=0, tiled=True
    ).astype(conv.dtype)
    gated = (query * returned).astype(jnp.bfloat16)
    terms = jnp.einsum(
        "cr,nc->rn",
        gated,
        lax.all_gather(out_weight, "seq", axis=0, tiled=True),
        preferred_element_type=jnp.float32,
    )
    summed = lax.psum_scatter(
        terms.astype(jnp.bfloat16), "tensor", scatter_dimension=1, tiled=True
    ).astype(jnp.float32)
    return residual_in + summed


def moved_shards(residual_in, norm_gain, in_weight, short_taps, long_filter, out_weight):
    length = lax.axis_size("seq")
    swap = [(i * length + j, j * length + i) for i in range(length) for j in range(length)]
    seq_index = lax.axis_index("seq")
    width = in_weight.shape[1]
    channels = long_filter.shape[0]
    block = lax.ppermute(residual_in.astype(jnp.bfloat16), ("seq", "tensor"), swap)
    features = lax.all_gather(block, "tensor", axis=0, tiled=True).astype(jnp.float32)
    squares = lax.psum(jnp.sum(features * features, axis=1), "seq")
    scale = lax.rsqrt(squares / norm_gain.shape[0] + EPSILON)
    gain = lax.dynamic_slice_in_dim(norm_gain, seq_index * width, width)
    partial = jnp.einsum(
        "rd,sdc->scr",
        (features * gain).astype(jnp.bfloat16),
        in_weight,
        preferred_element_type=jnp.float32,
    )
    projected = lax.psum_scatter(
        partial.astype(jnp.bfloat16), "seq", scatter_dimension=1, tiled=True
    ).astype(jnp.float32) * scale
    taps = lax.dynamic_slice_in_dim(short_taps, seq_index * channels, channels, axis=2)
    row_count = projected.shape[2]
    reach = taps.shape[1] - 1
    extended = jnp.pad(projected, ((0, 0), (0, 0), (reach, 0)))
    mixed = taps[:, 0, :, None] * projected
    for offset in range(1, reach + 1):
        mixed = (
            mixed
            + taps[:, offset, :, None]
            * extended[:, :, reach - offset : reach - offset + row_count]
        )
    query = mixed[0]
    by_channel = mixed[1] * mixed[2]
    full_length = 2 * by_channel.shape[1]
    low_factor, high_factor = split_length(full_length)
    cos_high, sin_high = angle_tables(high_factor, high_factor // 2, high_factor)
    cos_twist, sin_twist = angle_tables(full_length, low_factor, high_factor)
    cos_low, sin_low = angle_tables(low_factor, low_factor, low_factor)
    all_tables = (cos_high, sin_high, cos_twist, sin_twist, cos_low, sin_low)
    signal_real, signal_imag = forward_spectrum(by_channel, low_factor, high_factor, all_tables)
    filter_real, filter_imag = forward_spectrum(long_filter, low_factor, high_factor, all_tables)
    conv = inverse_signal(
        signal_real * filter_real - signal_imag * filter_imag,
        signal_real * filter_imag + signal_imag * filter_real,
        low_factor,
        high_factor,
        all_tables,
    )
    gated = lax.all_gather((query * conv).astype(jnp.bfloat16), "seq", axis=0, tiled=True)
    terms = jnp.einsum("cr,nc->rn", gated, out_weight, preferred_element_type=jnp.float32)
    summed = lax.psum_scatter(
        terms.astype(jnp.bfloat16), "tensor", scatter_dimension=0, tiled=True
    )
    returned = lax.ppermute(summed, ("seq", "tensor"), swap)
    return residual_in + returned.astype(jnp.float32)


def solution(mesh):
    body = moved_shards if mesh.shape["seq"] == mesh.shape["tensor"] else shards
    return jax.shard_map(
        body,
        mesh=mesh,
        in_specs=(
            P(("groups", "seq"), "tensor"),
            P(),
            P(None, "seq", "tensor"),
            P(None, None, "tensor"),
            P(("tensor", "seq"), None),
            P("seq", "tensor"),
        ),
        out_specs=P(("groups", "seq"), "tensor"),
        check_vma=False,
    )
```

```python
import math

import jax
import jax.numpy as jnp
import ml_dtypes
import numpy as np
from jax import lax
from jax.experimental import pallas as pl
from jax.experimental.pallas import tpu as pltpu
from jax.sharding import PartitionSpec as P

EPSILON = 1e-05


def shifted(value, axis, by):
    length = lax.axis_size(axis)
    pairs = [(i, i + by) for i in range(length) if 0 <= i + by < length]
    return lax.ppermute(value, axis, pairs)


def exact_product(form, left, right):
    return jnp.einsum(form, left, right, precision=lax.Precision.HIGHEST)


def angle_tables(modulus, count_a, count_b):
    index_a = jnp.arange(count_a, dtype=jnp.int32)[:, None]
    index_b = jnp.arange(count_b, dtype=jnp.int32)[None, :]
    theta = (index_a * index_b % modulus).astype(jnp.float32) * (2.0 * math.pi / modulus)
    return (jnp.cos(theta), jnp.sin(theta))


def split_length(full_length):
    low_factor = 1
    while full_length % (4 * low_factor) == 0 and 4 * low_factor * low_factor <= full_length:
        low_factor = low_factor * 2
    return (low_factor, full_length // low_factor)


def forward_spectrum(signal, low_factor, high_factor, all_tables):
    cos_high, sin_high, cos_twist, sin_twist, cos_low, sin_low = all_tables
    channel_count = signal.shape[0]
    blocks = signal.reshape(channel_count, high_factor // 2, low_factor)
    real_a = exact_product("cmp,mk->cpk", blocks, cos_high)
    imag_a = -exact_product("cmp,mk->cpk", blocks, sin_high)
    real_b = real_a * cos_twist + imag_a * sin_twist
    imag_b = imag_a * cos_twist - real_a * sin_twist
    real_x = exact_product("cpk,pj->cjk", real_b, cos_low) + exact_product(
        "cpk,pj->cjk", imag_b, sin_low
    )
    imag_x = exact_product("cpk,pj->cjk", imag_b, cos_low) - exact_product(
        "cpk,pj->cjk", real_b, sin_low
    )
    return (real_x, imag_x)


def inverse_signal(real_x, imag_x, low_factor, high_factor, all_tables):
    cos_high, sin_high, cos_twist, sin_twist, cos_low, sin_low = all_tables
    channel_count = real_x.shape[0]
    real_b = exact_product("cjk,pj->cpk", real_x, cos_low) - exact_product(
        "cjk,pj->cpk", imag_x, sin_low
    )
    imag_b = exact_product("cjk,pj->cpk", real_x, sin_low) + exact_product(
        "cjk,pj->cpk", imag_x, cos_low
    )
    real_c = real_b * cos_twist - imag_b * sin_twist
    imag_c = real_b * sin_twist + imag_b * cos_twist
    result = exact_product("cpk,mk->cmp", real_c, cos_high) - exact_product(
        "cpk,mk->cmp", imag_c, sin_high
    )
    full_length = low_factor * high_factor
    return (result / full_length).reshape(channel_count, full_length // 2)


def shards(residual_in, norm_gain, in_weight, short_taps, long_filter, out_weight):
    row_count, local_width = residual_in.shape
    full_rows = lax.all_gather(
        residual_in.astype(jnp.bfloat16), "tensor", axis=1, tiled=True
    ).astype(residual_in.dtype)
    mean_sq = jnp.mean(full_rows * full_rows, axis=1, keepdims=True)
    normed = (full_rows * lax.rsqrt(mean_sq + EPSILON) * norm_gain).astype(jnp.bfloat16)
    projected = jnp.einsum(
        "rd,sdc->scr",
        normed,
        lax.all_gather(in_weight, "seq", axis=1, tiled=True),
        preferred_element_type=jnp.float32,
    )
    reach = short_taps.shape[1] - 1
    earlier = shifted(projected[:, :, row_count - reach :], "seq", 1)
    extended = jnp.concatenate([earlier, projected], axis=2)
    mixed = short_taps[:, 0, :, None] * projected
    for offset in range(1, reach + 1):
        mixed = (
            mixed
            + short_taps[:, offset, :, None]
            * extended[:, :, reach - offset : reach - offset + row_count]
        )
    query = mixed[0]
    product_kv = mixed[1] * mixed[2]
    by_channel = lax.all_to_all(
        product_kv.astype(jnp.bfloat16), "seq", split_axis=0, concat_axis=1, tiled=True
    ).astype(product_kv.dtype)
    full_length = 2 * by_channel.shape[1]
    low_factor, high_factor = split_length(full_length)
    cos_high, sin_high = angle_tables(high_factor, high_factor // 2, high_factor)
    cos_twist, sin_twist = angle_tables(full_length, low_factor, high_factor)
    cos_low, sin_low = angle_tables(low_factor, low_factor, low_factor)
    all_tables = (cos_high, sin_high, cos_twist, sin_twist, cos_low, sin_low)
    signal_real, signal_imag = forward_spectrum(by_channel, low_factor, high_factor, all_tables)
    filter_real, filter_imag = forward_spectrum(long_filter, low_factor, high_factor, all_tables)
    conv = inverse_signal(
        signal_real * filter_real - signal_imag * filter_imag,
        signal_real * filter_imag + signal_imag * filter_real,
        low_factor,
        high_factor,
        all_tables,
    )
    returned = lax.all_to_all(
        conv.astype(jnp.bfloat16), "seq", split_axis=1, concat_axis=0, tiled=True
    ).astype(conv.dtype)
    gated = (query * returned).astype(jnp.bfloat16)
    terms = jnp.einsum(
        "cr,nc->rn",
        gated,
        lax.all_gather(out_weight, "seq", axis=0, tiled=True),
        preferred_element_type=jnp.float32,
    )
    summed = lax.psum_scatter(
        terms.astype(jnp.bfloat16), "tensor", scatter_dimension=1, tiled=True
    ).astype(jnp.float32)
    return residual_in + summed


MESH = pl.DeviceIdType.MESH


def transform_tables(length):
    index = np.arange(length)
    turns = ((2 * index[:, None] + 1) * index[None, :]) % (4 * length)
    theta = turns.astype(np.float64) * (math.pi / (2 * length))
    table = np.concatenate([np.cos(theta), np.sin(theta)], axis=0).astype(np.float32)
    high = table.astype(ml_dtypes.bfloat16)
    low = (table - high.astype(np.float32)).astype(ml_dtypes.bfloat16)
    return (high, low, np.ascontiguousarray(high.T), np.ascontiguousarray(low.T))


def two_parts(value):
    high = value.astype(jnp.bfloat16)
    low = (value - high.astype(jnp.float32)).astype(jnp.bfloat16)
    return (high, low)


def matmul(left, right):
    return jnp.dot(left, right, preferred_element_type=jnp.float32)


def matmul_nt(left, right):
    return lax.dot_general(left, right, (((1,), (1,)), ((), ())), preferred_element_type=jnp.float32)


def block_kernel(
    x_ref, gain_ref, w_hbm, taps_ref, filter_ref, wo_hbm, ah_hbm, al_hbm, bh_hbm, bl_hbm,
    out_ref,
    wv, wo, ah, al, bh, bl, xb, xg, part, sendb, from_low, from_high, squares, spectrum,
    gathered, terms, sibling_in, cross_in, final_in,
    load_sem, x_send, x_recv, p_send, low_recv, high_recv, q_send, q_recv,
    g_right, g_left, g_recv, t_send, t_recv,
):
    s = lax.axis_index("seq")
    t = lax.axis_index("tensor")
    n = 4
    rows, width = x_ref.shape
    ch = filter_ref.shape[0]
    length = filter_ref.shape[1]
    sib = t + 1 - 2 * lax.rem(t, 2)
    far = lax.rem(t + 2, n)
    far_sib = lax.rem(sib + 2, n)

    loads = []
    for d in range(n):
        for j in range(3):
            loads.append(pltpu.make_async_copy(
                w_hbm.at[j, :, pl.ds(d * ch, ch)],
                wv.at[d, :, pl.ds(j * ch, ch)],
                load_sem.at[d * 3 + j],
            ))
    for i, (source, target) in enumerate(
        ((ah_hbm, ah), (al_hbm, al), (wo_hbm, wo), (bh_hbm, bh), (bl_hbm, bl))
    ):
        loads.append(pltpu.make_async_copy(source, target, load_sem.at[3 * n + i]))
    for load in loads:
        load.start()

    barrier = pltpu.get_barrier_semaphore()
    for k in range(1, n):
        pl.semaphore_signal(barrier, inc=1, device_id={"seq": lax.rem(s + k, n), "tensor": t}, device_id_type=MESH)
        pl.semaphore_signal(barrier, inc=1, device_id={"seq": s, "tensor": lax.rem(t + k, n)}, device_id_type=MESH)

    @pl.when(s != t)
    def _():
        pl.semaphore_signal(barrier, inc=1, device_id={"seq": t, "tensor": s}, device_id_type=MESH)

    xb[...] = x_ref[...].astype(jnp.bfloat16)

    @pl.when(s != t)
    def _():
        pl.semaphore_wait(barrier, 2 * n - 1)

    @pl.when(s == t)
    def _():
        pl.semaphore_wait(barrier, 2 * n - 2)

    def remote(source, target, send, recv, to_s, to_t):
        return pltpu.make_async_remote_copy(
            src_ref=source, dst_ref=target, send_sem=send, recv_sem=recv,
            device_id={"seq": to_s, "tensor": to_t}, device_id_type=MESH,
        )

    swap = remote(xb, xg.at[s], x_send.at[0], x_recv.at[s], t, s)
    swapped = remote(xb, xg.at[t], x_send.at[0], x_recv.at[t], t, s)

    @pl.when(s != t)
    def _():
        swap.start()

    fh, fl = two_parts(filter_ref[...])
    loads[3 * n].wait()
    loads[3 * n + 1].wait()
    spectrum[...] = matmul_nt(ah[...], fh) + matmul_nt(ah[...], fl) + matmul_nt(al[...], fh)

    for load in loads[: 3 * n]:
        load.wait()

    @pl.when(s != t)
    def _():
        swapped.wait_recv()

    @pl.when(s == t)
    def _():
        xg[t] = xb[...]

    def slot_copy(slot, send, to_t):
        return remote(xg.at[slot], xg.at[slot], send, x_recv.at[slot], s, to_t)

    to_far = slot_copy(t, x_send.at[1], far)
    to_sib = slot_copy(t, x_send.at[2], sib)
    relay = slot_copy(far, x_send.at[3], sib)
    to_far.start()
    to_sib.start()

    gain = gain_ref[:, pl.ds(pl.multiple_of(s * width, 128), width)]
    ones = jnp.ones((8, width), jnp.bfloat16)

    def p_copy(p, d, up):
        target, recv = (from_low, low_recv) if up else (from_high, high_recv)
        return remote(
            sendb.at[p, d], target.at[p, d], p_send.at[p, d], recv.at[p, d],
            s + 1 if up else s - 1, t,
        )

    def dots(p):
        features = xg[p].astype(jnp.float32)
        sh, sl = two_parts(features * features)
        squares[s, :, pl.ds(pl.multiple_of(p * rows, 128), rows)] = matmul_nt(ones, sh) + matmul_nt(ones, sl)
        y = (features * gain).astype(jnp.bfloat16)

        @pl.loop(0, n)
        def _(d):
            part[p, d] = matmul(y, wv[d])

        @pl.when(s == 0)
        def _():
            @pl.loop(0, n - 1)
            def _(i):
                d = n - 1 - i
                sendb[p, d] = part[p, d].astype(jnp.bfloat16)
                p_copy(p, d, True).start()

        @pl.when(s == n - 1)
        def _():
            @pl.loop(0, n - 1)
            def _(d):
                sendb[p, d] = part[p, d].astype(jnp.bfloat16)
                p_copy(p, d, False).start()

    def chain(p):
        @pl.when((s > 0) & (s < n - 1))
        def _():
            @pl.loop(0, n - 1)
            def _(i):
                d = n - 1 - i

                @pl.when(d > s)
                def _():
                    p_copy(p, d, True).wait_recv()
                    sendb[p, d] = (part[p, d] + from_low[p, d].astype(jnp.float32)).astype(jnp.bfloat16)
                    p_copy(p, d, True).start()

                @pl.when(i < s)
                def _():
                    p_copy(p, i, False).wait_recv()
                    sendb[p, i] = (part[p, i] + from_high[p, i].astype(jnp.float32)).astype(jnp.bfloat16)
                    p_copy(p, i, False).start()

    dots(t)
    slot_copy(sib, x_send.at[2], sib).wait_recv()
    dots(sib)
    slot_copy(far, x_send.at[1], far).wait_recv()
    relay.start()
    dots(far)
    chain(t)
    slot_copy(far_sib, x_send.at[3], sib).wait_recv()
    dots(far_sib)

    q_copies = []
    for k in range(1, n):
        q_copy = remote(squares.at[s], squares.at[s], q_send.at[k], q_recv.at[s], lax.rem(s + k, n), t)
        q_copy.start()
        q_copies.append(q_copy)
    chain(sib)
    chain(far)
    chain(far_sib)

    for k in range(1, n):
        other = lax.rem(s + k, n)
        remote(squares.at[other], squares.at[other], q_send.at[k], q_recv.at[other], other, t).wait_recv()
    total = squares[0] + squares[1] + squares[2] + squares[3]
    scale = lax.rsqrt(total * (1.0 / (n * width)) + EPSILON)
    scale = jnp.transpose(jnp.broadcast_to(scale[0:1], (ch, length)))

    for p in (t, sib, far, far_sib):
        @pl.when(s > 0)
        def _():
            p_copy(p, s, True).wait_recv()
            part[p, s] += from_low[p, s].astype(jnp.float32)

        @pl.when(s < n - 1)
        def _():
            p_copy(p, s, False).wait_recv()
            part[p, s] += from_high[p, s].astype(jnp.float32)

    row = lax.broadcasted_iota(jnp.int32, (length, ch), 0)
    mixed = []
    for j in range(3):
        projected = jnp.concatenate([part[p, s, :, j * ch:(j + 1) * ch] for p in range(n)], axis=0) * scale
        taps = [taps_ref[j, o:o + 1, pl.ds(pl.multiple_of(s * ch, 128), ch)] for o in range(3)]
        value = taps[0] * projected
        for o in range(1, 3):
            value = value + taps[o] * jnp.where(row >= o, pltpu.roll(projected, o, 0), 0.0)
        mixed.append(value)
    query = mixed[0]
    kh, kl = two_parts(mixed[1] * mixed[2])
    both = matmul(ah[...], jnp.concatenate([kh, kl], axis=1))
    signal = both[:, :ch] + both[:, ch:] + matmul(al[...], kh)
    a, b = signal[:length], signal[length:]
    c, e = spectrum[:length], spectrum[length:]
    yh, yl = two_parts(jnp.concatenate([a * c - b * e, a * e + b * c], axis=0))
    for load in loads[3 * n + 2:]:
        load.wait()
    both = matmul(bh[...], jnp.concatenate([yh, yl], axis=1))
    conv = (both[:, :ch] + both[:, ch:] + matmul(bl[...], yh)) * (1.0 / length)

    def lanes(i):
        return pl.ds(pl.multiple_of(i * ch, 128), ch)

    gathered[:, lanes(s)] = (query * conv).astype(jnp.bfloat16)

    def g_copy(i, up):
        sems = g_right if up else g_left
        return remote(
            gathered.at[:, lanes(i)], gathered.at[:, lanes(i)], sems.at[i], g_recv.at[i],
            s + 1 if up else s - 1, t,
        )

    @pl.when(s < n - 1)
    def _():
        g_copy(s, True).start()

    @pl.when(s > 0)
    def _():
        g_copy(s, False).start()

    for k in range(1, n):
        @pl.when(s - k >= 0)
        def _():
            g_copy(s - k, True).wait_recv()

            @pl.when(s < n - 1)
            def _():
                g_copy(s - k, True).start()

        @pl.when(s + k < n)
        def _():
            g_copy(s + k, False).wait_recv()

            @pl.when(s > 0)
            def _():
                g_copy(s + k, False).start()

    def term(p):
        return matmul_nt(gathered[pl.ds(pl.multiple_of(p * rows, 128), rows), :], wo[...])

    far_out = remote(terms.at[0], sibling_in.at[0], t_send.at[0], t_recv.at[0], s, sib)
    own_out = remote(terms.at[1], sibling_in.at[1], t_send.at[1], t_recv.at[1], s, sib)
    cross = remote(terms.at[2], cross_in, t_send.at[2], t_recv.at[2], s, far)
    final = remote(terms.at[3], final_in, t_send.at[3], t_recv.at[3], t, s)
    terms[0] = term(far_sib).astype(jnp.bfloat16)
    far_out.start()
    terms[1] = term(sib).astype(jnp.bfloat16)
    own_out.start()
    far_term = term(far)
    far_out.wait_recv()
    terms[2] = (far_term + sibling_in[0].astype(jnp.float32)).astype(jnp.bfloat16)
    cross.start()
    own_term = term(t)
    own_out.wait_recv()
    own_term = own_term + sibling_in[1].astype(jnp.float32)
    cross.wait_recv()
    own_term = own_term + cross_in[...].astype(jnp.float32)

    @pl.when(s != t)
    def _():
        terms[3] = own_term.astype(jnp.bfloat16)
        final.start()
        final.wait_recv()
        out_ref[...] = x_ref[...] + final_in[...].astype(jnp.float32)

    @pl.when(s == t)
    def _():
        out_ref[...] = x_ref[...] + own_term

    @pl.when(s != t)
    def _():
        swap.wait_send()
        final.wait_send()

    for copy in [to_far, to_sib, relay, far_out, own_out, cross] + q_copies:
        copy.wait_send()
    for p in (t, sib, far, far_sib):
        @pl.loop(0, n)
        def _(d):
            @pl.when(d > s)
            def _():
                p_copy(p, d, True).wait_send()

            @pl.when(d < s)
            def _():
                p_copy(p, d, False).wait_send()

    @pl.loop(0, n)
    def _(i):
        @pl.when((i <= s) & (s < n - 1))
        def _():
            g_copy(i, True).wait_send()

        @pl.when((i >= s) & (s > 0))
        def _():
            g_copy(i, False).wait_send()


def kernel_shards(residual_in, norm_gain, in_weight, short_taps, long_filter, out_weight):
    n = 4
    rows, width = residual_in.shape
    ch, length = long_filter.shape
    tables = [jnp.asarray(table) for table in transform_tables(length)]
    vmem, hbm = pl.BlockSpec(memory_space=pltpu.VMEM), pl.BlockSpec(memory_space=pl.ANY)
    dma = pltpu.SemaphoreType.DMA
    bf16, f32 = jnp.bfloat16, jnp.float32
    return pl.pallas_call(
        block_kernel,
        out_shape=jax.ShapeDtypeStruct((rows, width), f32),
        in_specs=[vmem, vmem, hbm, vmem, vmem] + [hbm] * 5,
        out_specs=vmem,
        scratch_shapes=[
            pltpu.VMEM((n, width, 3 * ch), bf16),
            pltpu.VMEM(out_weight.shape, bf16),
            pltpu.VMEM((2 * length, length), bf16),
            pltpu.VMEM((2 * length, length), bf16),
            pltpu.VMEM((length, 2 * length), bf16),
            pltpu.VMEM((length, 2 * length), bf16),
            pltpu.VMEM((rows, width), bf16),
            pltpu.VMEM((n, rows, width), bf16),
            pltpu.VMEM((n, n, rows, 3 * ch), f32),
            pltpu.VMEM((n, n, rows, 3 * ch), bf16),
            pltpu.VMEM((n, n, rows, 3 * ch), bf16),
            pltpu.VMEM((n, n, rows, 3 * ch), bf16),
            pltpu.VMEM((n, 8, length), f32),
            pltpu.VMEM((2 * length, ch), f32),
            pltpu.VMEM((length, n * ch), bf16),
            pltpu.VMEM((n, rows, width), bf16),
            pltpu.VMEM((2, rows, width), bf16),
            pltpu.VMEM((rows, width), bf16),
            pltpu.VMEM((rows, width), bf16),
            dma((3 * n + 5,)), dma((n,)), dma((n,)), dma((n, n)), dma((n, n)), dma((n, n)),
            dma((n,)), dma((n,)), dma((n,)), dma((n,)), dma((n,)), dma((n,)), dma((n,)),
        ],
        compiler_params=pltpu.CompilerParams(
            collective_id=0, has_side_effects=True, vmem_limit_bytes=48 * 1024 * 1024
        ),
    )(residual_in, norm_gain[None], in_weight, short_taps, long_filter, out_weight, *tables)


def solution(mesh):
    square = mesh.shape["seq"] == 4 and mesh.shape["tensor"] == 4
    return jax.shard_map(
        kernel_shards if square else shards,
        mesh=mesh,
        in_specs=(
            P(("groups", "seq"), "tensor"),
            P(),
            P(None, "seq", "tensor"),
            P(None, None, "tensor"),
            P(("tensor", "seq"), None),
            P("seq", "tensor"),
        ),
        out_specs=P(("groups", "seq"), "tensor"),
        check_vma=False,
    )
```

```python
import math

import jax
import jax.numpy as jnp
import ml_dtypes
import numpy as np
from jax import lax
from jax.experimental import pallas as pl
from jax.experimental.pallas import tpu as pltpu
from jax.sharding import PartitionSpec as P

EPSILON = 1e-05


def shifted(value, axis, by):
    length = lax.axis_size(axis)
    pairs = [(i, i + by) for i in range(length) if 0 <= i + by < length]
    return lax.ppermute(value, axis, pairs)


def exact_product(form, left, right):
    return jnp.einsum(form, left, right, precision=lax.Precision.HIGHEST)


def angle_tables(modulus, count_a, count_b):
    index_a = jnp.arange(count_a, dtype=jnp.int32)[:, None]
    index_b = jnp.arange(count_b, dtype=jnp.int32)[None, :]
    theta = (index_a * index_b % modulus).astype(jnp.float32) * (2.0 * math.pi / modulus)
    return (jnp.cos(theta), jnp.sin(theta))


def split_length(full_length):
    low_factor = 1
    while full_length % (4 * low_factor) == 0 and 4 * low_factor * low_factor <= full_length:
        low_factor = low_factor * 2
    return (low_factor, full_length // low_factor)


def forward_spectrum(signal, low_factor, high_factor, all_tables):
    cos_high, sin_high, cos_twist, sin_twist, cos_low, sin_low = all_tables
    channel_count = signal.shape[0]
    blocks = signal.reshape(channel_count, high_factor // 2, low_factor)
    real_a = exact_product("cmp,mk->cpk", blocks, cos_high)
    imag_a = -exact_product("cmp,mk->cpk", blocks, sin_high)
    real_b = real_a * cos_twist + imag_a * sin_twist
    imag_b = imag_a * cos_twist - real_a * sin_twist
    real_x = exact_product("cpk,pj->cjk", real_b, cos_low) + exact_product(
        "cpk,pj->cjk", imag_b, sin_low
    )
    imag_x = exact_product("cpk,pj->cjk", imag_b, cos_low) - exact_product(
        "cpk,pj->cjk", real_b, sin_low
    )
    return (real_x, imag_x)


def inverse_signal(real_x, imag_x, low_factor, high_factor, all_tables):
    cos_high, sin_high, cos_twist, sin_twist, cos_low, sin_low = all_tables
    channel_count = real_x.shape[0]
    real_b = exact_product("cjk,pj->cpk", real_x, cos_low) - exact_product(
        "cjk,pj->cpk", imag_x, sin_low
    )
    imag_b = exact_product("cjk,pj->cpk", real_x, sin_low) + exact_product(
        "cjk,pj->cpk", imag_x, cos_low
    )
    real_c = real_b * cos_twist - imag_b * sin_twist
    imag_c = real_b * sin_twist + imag_b * cos_twist
    result = exact_product("cpk,mk->cmp", real_c, cos_high) - exact_product(
        "cpk,mk->cmp", imag_c, sin_high
    )
    full_length = low_factor * high_factor
    return (result / full_length).reshape(channel_count, full_length // 2)


def shards(residual_in, norm_gain, in_weight, short_taps, long_filter, out_weight):
    row_count, local_width = residual_in.shape
    full_rows = lax.all_gather(
        residual_in.astype(jnp.bfloat16), "tensor", axis=1, tiled=True
    ).astype(residual_in.dtype)
    mean_sq = jnp.mean(full_rows * full_rows, axis=1, keepdims=True)
    normed = (full_rows * lax.rsqrt(mean_sq + EPSILON) * norm_gain).astype(jnp.bfloat16)
    projected = jnp.einsum(
        "rd,sdc->scr",
        normed,
        lax.all_gather(in_weight, "seq", axis=1, tiled=True),
        preferred_element_type=jnp.float32,
    )
    reach = short_taps.shape[1] - 1
    earlier = shifted(projected[:, :, row_count - reach :], "seq", 1)
    extended = jnp.concatenate([earlier, projected], axis=2)
    mixed = short_taps[:, 0, :, None] * projected
    for offset in range(1, reach + 1):
        mixed = (
            mixed
            + short_taps[:, offset, :, None]
            * extended[:, :, reach - offset : reach - offset + row_count]
        )
    query = mixed[0]
    product_kv = mixed[1] * mixed[2]
    by_channel = lax.all_to_all(
        product_kv.astype(jnp.bfloat16), "seq", split_axis=0, concat_axis=1, tiled=True
    ).astype(product_kv.dtype)
    full_length = 2 * by_channel.shape[1]
    low_factor, high_factor = split_length(full_length)
    cos_high, sin_high = angle_tables(high_factor, high_factor // 2, high_factor)
    cos_twist, sin_twist = angle_tables(full_length, low_factor, high_factor)
    cos_low, sin_low = angle_tables(low_factor, low_factor, low_factor)
    all_tables = (cos_high, sin_high, cos_twist, sin_twist, cos_low, sin_low)
    signal_real, signal_imag = forward_spectrum(by_channel, low_factor, high_factor, all_tables)
    filter_real, filter_imag = forward_spectrum(long_filter, low_factor, high_factor, all_tables)
    conv = inverse_signal(
        signal_real * filter_real - signal_imag * filter_imag,
        signal_real * filter_imag + signal_imag * filter_real,
        low_factor,
        high_factor,
        all_tables,
    )
    returned = lax.all_to_all(
        conv.astype(jnp.bfloat16), "seq", split_axis=1, concat_axis=0, tiled=True
    ).astype(conv.dtype)
    gated = (query * returned).astype(jnp.bfloat16)
    terms = jnp.einsum(
        "cr,nc->rn",
        gated,
        lax.all_gather(out_weight, "seq", axis=0, tiled=True),
        preferred_element_type=jnp.float32,
    )
    summed = lax.psum_scatter(
        terms.astype(jnp.bfloat16), "tensor", scatter_dimension=1, tiled=True
    ).astype(jnp.float32)
    return residual_in + summed


MESH = pl.DeviceIdType.MESH


def transform_tables(length):
    index = np.arange(length)
    turns = ((2 * index[:, None] + 1) * index[None, :]) % (4 * length)
    theta = turns.astype(np.float64) * (math.pi / (2 * length))
    table = np.concatenate([np.cos(theta), np.sin(theta)], axis=0).astype(np.float32)
    high = table.astype(ml_dtypes.bfloat16)
    low = (table - high.astype(np.float32)).astype(ml_dtypes.bfloat16)
    return (high, low, np.ascontiguousarray(high.T), np.ascontiguousarray(low.T))


def two_parts(value):
    high = value.astype(jnp.bfloat16)
    low = (value - high.astype(jnp.float32)).astype(jnp.bfloat16)
    return (high, low)


def matmul(left, right):
    return jnp.dot(left, right, preferred_element_type=jnp.float32)


def matmul_nt(left, right):
    return lax.dot_general(left, right, (((1,), (1,)), ((), ())), preferred_element_type=jnp.float32)


def block_kernel(
    x_hbm, gain_hbm, w_hbm, taps_hbm, filter_hbm, wo_hbm, ah_hbm, al_hbm, bh_hbm, bl_hbm,
    out_ref,
    x_ref, gain_ref, taps_ref, filter_ref, wv, wo, ah, al, bh, bl, xb, xg, part, sendb, from_low, from_high, squares, spectrum,
    gathered, terms, terms_acc, sibling_in, cross_in, final_in,
    load_sem, x_send, x_recv, p_send, low_recv, high_recv, q_send, q_recv,
    g_right, g_left, g_recv, t_send, t_recv,
):
    s = lax.axis_index("seq")
    t = lax.axis_index("tensor")
    n = 4
    rows, width = x_ref.shape
    ch = filter_ref.shape[0]
    length = filter_ref.shape[1]
    sib = t + 1 - 2 * lax.rem(t, 2)
    far = lax.rem(t + 2, n)
    far_sib = lax.rem(sib + 2, n)

    chunks = 4
    step = rows // chunks

    def lanes(i):
        return pl.ds(pl.multiple_of(i * ch, 128), ch)

    loads = []
    for d in range(n):
        for j in range(3):
            loads.append(pltpu.make_async_copy(
                w_hbm.at[(j + 1) % 3, :, pl.ds(d * ch, ch)],
                wv.at[d, :, pl.ds(j * ch, ch)],
                load_sem.at[d * 3 + j],
            ))
    for i, (source, target) in enumerate((
        (ah_hbm, ah), (al_hbm, al), (wo_hbm, wo), (bh_hbm, bh), (bl_hbm, bl),
        (x_hbm, x_ref), (filter_hbm, filter_ref), (taps_hbm.at[:, :, lanes(s)], taps_ref),
        (gain_hbm.at[:, pl.ds(pl.multiple_of(s * width, 128), width)], gain_ref),
    )):
        loads.append(pltpu.make_async_copy(source, target, load_sem.at[3 * n + i]))
    x_load, filter_load, taps_load, gain_load = loads[3 * n + 5:]
    x_load.start()

    barrier = pltpu.get_barrier_semaphore()
    for k in range(1, n):
        pl.semaphore_signal(barrier, inc=1, device_id={"seq": lax.rem(s + k, n), "tensor": t}, device_id_type=MESH)
        pl.semaphore_signal(barrier, inc=1, device_id={"seq": s, "tensor": lax.rem(t + k, n)}, device_id_type=MESH)

    @pl.when(s != t)
    def _():
        pl.semaphore_signal(barrier, inc=1, device_id={"seq": t, "tensor": s}, device_id_type=MESH)

    filter_load.start()
    for load in loads[3 * n:3 * n + 2] + loads[:3 * n] + [gain_load, taps_load] + loads[3 * n + 2:3 * n + 5]:
        load.start()
    x_load.wait()
    xb[...] = x_ref[...].astype(jnp.bfloat16)

    @pl.when(s != t)
    def _():
        pl.semaphore_wait(barrier, 2 * n - 1)

    @pl.when(s == t)
    def _():
        pl.semaphore_wait(barrier, 2 * n - 2)

    def remote(source, target, send, recv, to_s, to_t):
        return pltpu.make_async_remote_copy(
            src_ref=source, dst_ref=target, send_sem=send, recv_sem=recv,
            device_id={"seq": to_s, "tensor": to_t}, device_id_type=MESH,
        )

    def piece(h):
        return pl.ds(h * step, step)

    def swap(h, slot):
        return remote(
            xb.at[piece(h)], xg.at[slot, piece(h)], x_send.at[0, h], x_recv.at[slot, h], t, s
        )

    @pl.when(s != t)
    def _():
        for h in range(chunks):
            swap(h, s).start()

    filter_load.wait()
    fh, fl = two_parts(filter_ref[...])
    loads[3 * n].wait()
    loads[3 * n + 1].wait()
    spectrum[...] = matmul_nt(ah[...], fh) + matmul_nt(ah[...], fl) + matmul_nt(al[...], fh)

    def slot_copy(slot, which, to_t, h):
        return remote(
            xg.at[slot, piece(h)], xg.at[slot, piece(h)], x_send.at[which, h], x_recv.at[slot, h], s, to_t
        )

    @pl.when(s == t)
    def _():
        xg[t] = xb[...]

    for h in range(chunks):
        @pl.when(s != t)
        def _():
            swap(h, t).wait_recv()

        slot_copy(t, 1, far, h).start()
        slot_copy(t, 2, sib, h).start()

    for load in loads[: 3 * n]:
        load.wait()
    gain_load.wait()
    gain = gain_ref[...]
    ones = jnp.ones((8, width), jnp.bfloat16)

    cuts = (slice(0, 2 * ch), slice(2 * ch, 3 * ch))

    def p_copy(p, d, up, q):
        target, recv = (from_low, low_recv) if up else (from_high, high_recv)
        return remote(
            sendb.at[p, d, :, cuts[q]], target.at[p, d, :, cuts[q]], p_send.at[q, p, d], recv.at[q, p, d],
            s + 1 if up else s - 1, t,
        )

    def first(p, q):
        @pl.when(s == 0)
        def _():
            @pl.loop(0, n - 1)
            def _(i):
                d = n - 1 - i
                sendb[p, d, :, cuts[q]] = part[p, d, :, cuts[q]].astype(jnp.bfloat16)
                p_copy(p, d, True, q).start()

        @pl.when(s == n - 1)
        def _():
            @pl.loop(0, n - 1)
            def _(d):
                sendb[p, d, :, cuts[q]] = part[p, d, :, cuts[q]].astype(jnp.bfloat16)
                p_copy(p, d, False, q).start()

    def dots(p):
        features = xg[p].astype(jnp.float32)
        sh, sl = two_parts(features * features)
        squares[s, :, pl.ds(pl.multiple_of(p * rows, 128), rows)] = matmul_nt(ones, sh) + matmul_nt(ones, sl)
        y = (features * gain).astype(jnp.bfloat16)

        @pl.loop(0, n)
        def _(d):
            part[p, d] = matmul(y, wv[d])

    def chain(p, q):
        @pl.when((s > 0) & (s < n - 1))
        def _():
            @pl.loop(0, n - 1)
            def _(i):
                d = n - 1 - i

                @pl.when(d > s)
                def _():
                    p_copy(p, d, True, q).wait_recv()
                    sendb[p, d, :, cuts[q]] = (
                        part[p, d, :, cuts[q]] + from_low[p, d, :, cuts[q]].astype(jnp.float32)
                    ).astype(jnp.bfloat16)
                    p_copy(p, d, True, q).start()

                @pl.when(i < s)
                def _():
                    p_copy(p, i, False, q).wait_recv()
                    sendb[p, i, :, cuts[q]] = (
                        part[p, i, :, cuts[q]] + from_high[p, i, :, cuts[q]].astype(jnp.float32)
                    ).astype(jnp.bfloat16)
                    p_copy(p, i, False, q).start()

    def total(p, q):
        @pl.when(s > 0)
        def _():
            p_copy(p, s, True, q).wait_recv()
            part[p, s, :, cuts[q]] += from_low[p, s, :, cuts[q]].astype(jnp.float32)

        @pl.when(s < n - 1)
        def _():
            p_copy(p, s, False, q).wait_recv()
            part[p, s, :, cuts[q]] += from_high[p, s, :, cuts[q]].astype(jnp.float32)

    order = (t, sib, far, far_sib)
    dots(t)
    first(t, 0)
    for h in range(chunks):
        slot_copy(far, 1, far, h).wait_recv()
        slot_copy(far, 3, sib, h).start()
    for h in range(chunks):
        slot_copy(sib, 2, sib, h).wait_recv()
    dots(sib)
    first(sib, 0)
    dots(far)
    first(far, 0)
    chain(t, 0)
    for h in range(chunks):
        slot_copy(far_sib, 3, sib, h).wait_recv()
    dots(far_sib)
    first(far_sib, 0)

    q_copies = []
    for k in range(1, n):
        q_copy = remote(squares.at[s], squares.at[s], q_send.at[k], q_recv.at[s], lax.rem(s + k, n), t)
        q_copy.start()
        q_copies.append(q_copy)
    for p in order:
        first(p, 1)
    for p in order[1:]:
        chain(p, 0)

    for k in range(1, n):
        other = lax.rem(s + k, n)
        remote(squares.at[other], squares.at[other], q_send.at[k], q_recv.at[other], other, t).wait_recv()
    all_squares = squares[0] + squares[1] + squares[2] + squares[3]
    scale = lax.rsqrt(all_squares * (1.0 / (n * width)) + EPSILON)
    scale = jnp.transpose(jnp.broadcast_to(scale[0:1], (ch, length)))
    taps_load.wait()
    for p in order:
        total(p, 0)

    row = lax.broadcasted_iota(jnp.int32, (length, ch), 0)

    def filtered(j):
        at = (j + 2) % 3 * ch
        projected = jnp.concatenate([part[p, s, :, at:at + ch] for p in range(n)], axis=0) * scale
        taps = [taps_ref[j, o:o + 1, :] for o in range(3)]
        value = taps[0] * projected
        for o in range(1, 3):
            value = value + taps[o] * jnp.where(row >= o, pltpu.roll(projected, o, 0), 0.0)
        return value

    kh, kl = two_parts(filtered(1) * filtered(2))
    chain(order[0], 1)
    both = matmul(ah[...], jnp.concatenate([kh, kl], axis=1))
    signal = both[:, :ch] + both[:, ch:] + matmul(al[...], kh)
    chain(order[1], 1)
    a, b = signal[:length], signal[length:]
    c, e = spectrum[:length], spectrum[length:]
    yh, yl = two_parts(jnp.concatenate([a * c - b * e, a * e + b * c], axis=0))
    for load in loads[3 * n + 2:3 * n + 5]:
        load.wait()
    chain(order[2], 1)
    both = matmul(bh[...], jnp.concatenate([yh, yl], axis=1))
    conv = (both[:, :ch] + both[:, ch:] + matmul(bl[...], yh)) * (1.0 / length)
    chain(order[3], 1)
    for p in order:
        total(p, 1)
    query = filtered(0)

    gathered[:, lanes(s)] = (query * conv).astype(jnp.bfloat16)

    def g_copy(i, up):
        sems = g_right if up else g_left
        return remote(
            gathered.at[:, lanes(i)], gathered.at[:, lanes(i)], sems.at[i], g_recv.at[i],
            s + 1 if up else s - 1, t,
        )

    @pl.when(s < n - 1)
    def _():
        g_copy(s, True).start()

    @pl.when(s > 0)
    def _():
        g_copy(s, False).start()

    for k in range(1, n):
        @pl.when(s - k >= 0)
        def _():
            g_copy(s - k, True).wait_recv()

            @pl.when(s < n - 1)
            def _():
                g_copy(s - k, True).start()

        @pl.when(s + k < n)
        def _():
            g_copy(s + k, False).wait_recv()

            @pl.when(s > 0)
            def _():
                g_copy(s + k, False).start()

    def term(p):
        return matmul_nt(gathered[pl.ds(pl.multiple_of(p * rows, 128), rows), :], wo[...])

    def hop(which, target, to_s, to_t, h):
        return remote(
            terms.at[which, piece(h)], target.at[piece(h)], t_send.at[which, h], t_recv.at[which, h], to_s, to_t
        )

    def far_out(h):
        return hop(0, sibling_in.at[0], s, sib, h)

    def own_out(h):
        return hop(1, sibling_in.at[1], s, sib, h)

    def cross(h):
        return hop(2, cross_in, s, far, h)

    def final(h):
        return hop(3, final_in, t, s, h)

    terms[0] = term(far_sib).astype(jnp.bfloat16)
    for h in range(chunks):
        far_out(h).start()
    terms_acc[...] = term(far)
    for h in range(chunks):
        far_out(h).wait_recv()
        terms[2, piece(h)] = (
            terms_acc[piece(h)] + sibling_in[0, piece(h)].astype(jnp.float32)
        ).astype(jnp.bfloat16)
        cross(h).start()
    terms[1] = term(sib).astype(jnp.bfloat16)
    for h in range(chunks):
        own_out(h).start()
    terms_acc[...] = term(t)
    for h in range(chunks):
        own_out(h).wait_recv()
        terms_acc[piece(h)] += sibling_in[1, piece(h)].astype(jnp.float32)
    for h in range(chunks):
        cross(h).wait_recv()
        value = terms_acc[piece(h)] + cross_in[piece(h)].astype(jnp.float32)

        @pl.when(s != t)
        def _():
            terms[3, piece(h)] = value.astype(jnp.bfloat16)
            final(h).start()

        @pl.when(s == t)
        def _():
            out_ref[piece(h)] = x_ref[piece(h)] + value

    @pl.when(s != t)
    def _():
        for h in range(chunks):
            final(h).wait_recv()
            out_ref[piece(h)] = x_ref[piece(h)] + final_in[piece(h)].astype(jnp.float32)
        for h in range(chunks):
            swap(h, s).wait_send()
            final(h).wait_send()

    for h in range(chunks):
        for copy in (
            slot_copy(t, 1, far, h), slot_copy(t, 2, sib, h), slot_copy(far, 3, sib, h),
            far_out(h), own_out(h), cross(h),
        ):
            copy.wait_send()
    for copy in q_copies:
        copy.wait_send()
    for p in order:
        for q in range(2):
            @pl.loop(0, n)
            def _(d):
                @pl.when(d > s)
                def _():
                    p_copy(p, d, True, q).wait_send()

                @pl.when(d < s)
                def _():
                    p_copy(p, d, False, q).wait_send()

    @pl.loop(0, n)
    def _(i):
        @pl.when((i <= s) & (s < n - 1))
        def _():
            g_copy(i, True).wait_send()

        @pl.when((i >= s) & (s > 0))
        def _():
            g_copy(i, False).wait_send()


def kernel_shards(residual_in, norm_gain, in_weight, short_taps, long_filter, out_weight):
    n = 4
    rows, width = residual_in.shape
    ch, length = long_filter.shape
    tables = [jnp.asarray(table) for table in transform_tables(length)]
    vmem, hbm = pl.BlockSpec(memory_space=pltpu.VMEM), pl.BlockSpec(memory_space=pl.ANY)
    dma = pltpu.SemaphoreType.DMA
    bf16, f32 = jnp.bfloat16, jnp.float32
    return pl.pallas_call(
        block_kernel,
        out_shape=jax.ShapeDtypeStruct((rows, width), f32),
        in_specs=[hbm] * 10,
        out_specs=vmem,
        scratch_shapes=[
            pltpu.VMEM((rows, width), f32),
            pltpu.VMEM((1, width), f32),
            pltpu.VMEM(short_taps.shape[:2] + (ch,), f32),
            pltpu.VMEM((ch, length), f32),
            pltpu.VMEM((n, width, 3 * ch), bf16),
            pltpu.VMEM(out_weight.shape, bf16),
            pltpu.VMEM((2 * length, length), bf16),
            pltpu.VMEM((2 * length, length), bf16),
            pltpu.VMEM((length, 2 * length), bf16),
            pltpu.VMEM((length, 2 * length), bf16),
            pltpu.VMEM((rows, width), bf16),
            pltpu.VMEM((n, rows, width), bf16),
            pltpu.VMEM((n, n, rows, 3 * ch), f32),
            pltpu.VMEM((n, n, rows, 3 * ch), bf16),
            pltpu.VMEM((n, n, rows, 3 * ch), bf16),
            pltpu.VMEM((n, n, rows, 3 * ch), bf16),
            pltpu.VMEM((n, 8, length), f32),
            pltpu.VMEM((2 * length, ch), f32),
            pltpu.VMEM((length, n * ch), bf16),
            pltpu.VMEM((n, rows, width), bf16),
            pltpu.VMEM((rows, width), f32),
            pltpu.VMEM((2, rows, width), bf16),
            pltpu.VMEM((rows, width), bf16),
            pltpu.VMEM((rows, width), bf16),
            dma((3 * n + 9,)), dma((n, n)), dma((n, n)), dma((2, n, n)), dma((2, n, n)), dma((2, n, n)),
            dma((n,)), dma((n,)), dma((n,)), dma((n,)), dma((n,)), dma((n, n)), dma((n, n)),
        ],
        compiler_params=pltpu.CompilerParams(
            collective_id=0, has_side_effects=True, vmem_limit_bytes=60 * 1024 * 1024
        ),
    )(residual_in, norm_gain[None], in_weight, short_taps, long_filter, out_weight, *tables)


def solution(mesh):
    square = mesh.shape["seq"] == 4 and mesh.shape["tensor"] == 4
    return jax.shard_map(
        kernel_shards if square else shards,
        mesh=mesh,
        in_specs=(
            P(("groups", "seq"), "tensor"),
            P(),
            P(None, "seq", "tensor"),
            P(None, None, "tensor"),
            P(("tensor", "seq"), None),
            P("seq", "tensor"),
        ),
        out_specs=P(("groups", "seq"), "tensor"),
        check_vma=False,
    )
```

```python
import math

import jax
import jax.numpy as jnp
import ml_dtypes
import numpy as np
from jax import lax
from jax.experimental import pallas as pl
from jax.experimental.pallas import tpu as pltpu
from jax.sharding import PartitionSpec as P

EPSILON = 1e-05


def shifted(value, axis, by):
    length = lax.axis_size(axis)
    pairs = [(i, i + by) for i in range(length) if 0 <= i + by < length]
    return lax.ppermute(value, axis, pairs)


def exact_product(form, left, right):
    return jnp.einsum(form, left, right, precision=lax.Precision.HIGHEST)


def angle_tables(modulus, count_a, count_b):
    index_a = jnp.arange(count_a, dtype=jnp.int32)[:, None]
    index_b = jnp.arange(count_b, dtype=jnp.int32)[None, :]
    theta = (index_a * index_b % modulus).astype(jnp.float32) * (2.0 * math.pi / modulus)
    return (jnp.cos(theta), jnp.sin(theta))


def split_length(full_length):
    low_factor = 1
    while full_length % (4 * low_factor) == 0 and 4 * low_factor * low_factor <= full_length:
        low_factor = low_factor * 2
    return (low_factor, full_length // low_factor)


def forward_spectrum(signal, low_factor, high_factor, all_tables):
    cos_high, sin_high, cos_twist, sin_twist, cos_low, sin_low = all_tables
    channel_count = signal.shape[0]
    blocks = signal.reshape(channel_count, high_factor // 2, low_factor)
    real_a = exact_product("cmp,mk->cpk", blocks, cos_high)
    imag_a = -exact_product("cmp,mk->cpk", blocks, sin_high)
    real_b = real_a * cos_twist + imag_a * sin_twist
    imag_b = imag_a * cos_twist - real_a * sin_twist
    real_x = exact_product("cpk,pj->cjk", real_b, cos_low) + exact_product(
        "cpk,pj->cjk", imag_b, sin_low
    )
    imag_x = exact_product("cpk,pj->cjk", imag_b, cos_low) - exact_product(
        "cpk,pj->cjk", real_b, sin_low
    )
    return (real_x, imag_x)


def inverse_signal(real_x, imag_x, low_factor, high_factor, all_tables):
    cos_high, sin_high, cos_twist, sin_twist, cos_low, sin_low = all_tables
    channel_count = real_x.shape[0]
    real_b = exact_product("cjk,pj->cpk", real_x, cos_low) - exact_product(
        "cjk,pj->cpk", imag_x, sin_low
    )
    imag_b = exact_product("cjk,pj->cpk", real_x, sin_low) + exact_product(
        "cjk,pj->cpk", imag_x, cos_low
    )
    real_c = real_b * cos_twist - imag_b * sin_twist
    imag_c = real_b * sin_twist + imag_b * cos_twist
    result = exact_product("cpk,mk->cmp", real_c, cos_high) - exact_product(
        "cpk,mk->cmp", imag_c, sin_high
    )
    full_length = low_factor * high_factor
    return (result / full_length).reshape(channel_count, full_length // 2)


def shards(residual_in, norm_gain, in_weight, short_taps, long_filter, out_weight):
    row_count, local_width = residual_in.shape
    full_rows = lax.all_gather(
        residual_in.astype(jnp.bfloat16), "tensor", axis=1, tiled=True
    ).astype(residual_in.dtype)
    mean_sq = jnp.mean(full_rows * full_rows, axis=1, keepdims=True)
    normed = (full_rows * lax.rsqrt(mean_sq + EPSILON) * norm_gain).astype(jnp.bfloat16)
    projected = jnp.einsum(
        "rd,sdc->scr",
        normed,
        lax.all_gather(in_weight, "seq", axis=1, tiled=True),
        preferred_element_type=jnp.float32,
    )
    reach = short_taps.shape[1] - 1
    earlier = shifted(projected[:, :, row_count - reach :], "seq", 1)
    extended = jnp.concatenate([earlier, projected], axis=2)
    mixed = short_taps[:, 0, :, None] * projected
    for offset in range(1, reach + 1):
        mixed = (
            mixed
            + short_taps[:, offset, :, None]
            * extended[:, :, reach - offset : reach - offset + row_count]
        )
    query = mixed[0]
    product_kv = mixed[1] * mixed[2]
    by_channel = lax.all_to_all(
        product_kv.astype(jnp.bfloat16), "seq", split_axis=0, concat_axis=1, tiled=True
    ).astype(product_kv.dtype)
    full_length = 2 * by_channel.shape[1]
    low_factor, high_factor = split_length(full_length)
    cos_high, sin_high = angle_tables(high_factor, high_factor // 2, high_factor)
    cos_twist, sin_twist = angle_tables(full_length, low_factor, high_factor)
    cos_low, sin_low = angle_tables(low_factor, low_factor, low_factor)
    all_tables = (cos_high, sin_high, cos_twist, sin_twist, cos_low, sin_low)
    signal_real, signal_imag = forward_spectrum(by_channel, low_factor, high_factor, all_tables)
    filter_real, filter_imag = forward_spectrum(long_filter, low_factor, high_factor, all_tables)
    conv = inverse_signal(
        signal_real * filter_real - signal_imag * filter_imag,
        signal_real * filter_imag + signal_imag * filter_real,
        low_factor,
        high_factor,
        all_tables,
    )
    returned = lax.all_to_all(
        conv.astype(jnp.bfloat16), "seq", split_axis=1, concat_axis=0, tiled=True
    ).astype(conv.dtype)
    gated = (query * returned).astype(jnp.bfloat16)
    terms = jnp.einsum(
        "cr,nc->rn",
        gated,
        lax.all_gather(out_weight, "seq", axis=0, tiled=True),
        preferred_element_type=jnp.float32,
    )
    summed = lax.psum_scatter(
        terms.astype(jnp.bfloat16), "tensor", scatter_dimension=1, tiled=True
    ).astype(jnp.float32)
    return residual_in + summed


MESH = pl.DeviceIdType.MESH


def transform_tables(length):
    index = np.arange(length)
    turns = ((2 * index[:, None] + 1) * index[None, :]) % (4 * length)
    theta = turns.astype(np.float64) * (math.pi / (2 * length))
    table = np.concatenate([np.cos(theta), np.sin(theta)], axis=0).astype(np.float32)
    high = table.astype(ml_dtypes.bfloat16)
    low = (table - high.astype(np.float32)).astype(ml_dtypes.bfloat16)
    return (high, low, np.ascontiguousarray(high.T), np.ascontiguousarray(low.T))


def two_parts(value):
    high = value.astype(jnp.bfloat16)
    low = (value - high.astype(jnp.float32)).astype(jnp.bfloat16)
    return (high, low)


def matmul(left, right):
    return jnp.dot(left, right, preferred_element_type=jnp.float32)


def matmul_nt(left, right):
    return lax.dot_general(left, right, (((1,), (1,)), ((), ())), preferred_element_type=jnp.float32)


def block_kernel(
    x_hbm, gain_hbm, w_hbm, taps_hbm, filter_hbm, wo_hbm, ah_hbm, al_hbm, bh_hbm, bl_hbm,
    out_ref,
    x_ref, gain_ref, taps_ref, filter_ref, wv, wo, ah, al, bh, bl, xb, xg, part, send_kv, send_q, low_kv, low_q, high_kv, high_q, squares, spectrum,
    gathered, terms, terms_acc, sibling_in, cross_in, final_in,
    load_sem, x_send, x_recv, p_send, low_recv, high_recv, q_send, q_recv,
    g_right, g_left, g_recv, t_send, t_recv,
):
    s = lax.axis_index("seq")
    t = lax.axis_index("tensor")
    n = 4
    rows, width = x_ref.shape
    ch = filter_ref.shape[0]
    length = filter_ref.shape[1]
    sib = t + 1 - 2 * lax.rem(t, 2)
    far = lax.rem(t + 2, n)
    far_sib = lax.rem(sib + 2, n)

    chunks = 2
    step = rows // chunks

    def lanes(i):
        return pl.ds(pl.multiple_of(i * ch, 128), ch)

    loads = []
    for d in range(n):
        for j in range(3):
            loads.append(pltpu.make_async_copy(
                w_hbm.at[(j + 1) % 3, :, pl.ds(d * ch, ch)],
                wv.at[d, :, pl.ds(j * ch, ch)],
                load_sem.at[d * 3 + j],
            ))
    for i, (source, target) in enumerate((
        (ah_hbm, ah), (al_hbm, al), (wo_hbm, wo), (bh_hbm, bh), (bl_hbm, bl),
        (x_hbm, x_ref), (filter_hbm, filter_ref), (taps_hbm.at[:, :, lanes(s)], taps_ref),
        (gain_hbm.at[:, pl.ds(pl.multiple_of(s * width, 128), width)], gain_ref),
    )):
        loads.append(pltpu.make_async_copy(source, target, load_sem.at[3 * n + i]))
    x_load, filter_load, taps_load, gain_load = loads[3 * n + 5:]
    x_load.start()

    barrier = pltpu.get_barrier_semaphore()
    for k in range(1, n):
        pl.semaphore_signal(barrier, inc=1, device_id={"seq": lax.rem(s + k, n), "tensor": t}, device_id_type=MESH)
        pl.semaphore_signal(barrier, inc=1, device_id={"seq": s, "tensor": lax.rem(t + k, n)}, device_id_type=MESH)

    @pl.when(s != t)
    def _():
        pl.semaphore_signal(barrier, inc=1, device_id={"seq": t, "tensor": s}, device_id_type=MESH)

    x_load.wait()
    xb[...] = x_ref[...].astype(jnp.bfloat16)

    @pl.when(s != t)
    def _():
        pl.semaphore_wait(barrier, 2 * n - 1)

    @pl.when(s == t)
    def _():
        pl.semaphore_wait(barrier, 2 * n - 2)

    def remote(source, target, send, recv, to_s, to_t):
        return pltpu.make_async_remote_copy(
            src_ref=source, dst_ref=target, send_sem=send, recv_sem=recv,
            device_id={"seq": to_s, "tensor": to_t}, device_id_type=MESH,
        )

    def piece(h):
        return pl.ds(h * step, step)

    def swap(h, slot):
        return remote(
            xb.at[piece(h)], xg.at[slot, piece(h)], x_send.at[0, h], x_recv.at[slot, h], t, s
        )

    @pl.when(s != t)
    def _():
        for h in range(chunks):
            swap(h, s).start()

    gain_load.start()
    for load in loads[:3 * n] + [filter_load] + loads[3 * n:3 * n + 2] + [taps_load] + loads[3 * n + 2:3 * n + 5]:
        load.start()

    def slot_copy(slot, which, to_t, h):
        return remote(
            xg.at[slot, piece(h)], xg.at[slot, piece(h)], x_send.at[which, h], x_recv.at[slot, h], s, to_t
        )

    @pl.when(s == t)
    def _():
        xg[t] = xb[...]

    for h in range(chunks):
        @pl.when(s != t)
        def _():
            swap(h, t).wait_recv()

        slot_copy(t, 1, far, h).start()
        slot_copy(t, 2, sib, h).start()

    for load in loads[: 3 * n]:
        load.wait()
    gain_load.wait()
    gain = gain_ref[...]
    ones = jnp.ones((8, width), jnp.bfloat16)

    cuts = (slice(0, 2 * ch), slice(2 * ch, 3 * ch))
    sendb, from_low, from_high = (send_kv, send_q), (low_kv, low_q), (high_kv, high_q)

    def p_copy(p, d, up, q):
        target, recv = (from_low, low_recv) if up else (from_high, high_recv)
        return remote(
            sendb[q].at[p, d], target[q].at[p, d], p_send.at[q, p, d], recv.at[q, p, d],
            s + 1 if up else s - 1, t,
        )

    def first(p, q):
        @pl.when(s == 0)
        def _():
            @pl.loop(0, n - 1)
            def _(i):
                d = n - 1 - i
                sendb[q][p, d] = part[p, d, :, cuts[q]].astype(jnp.bfloat16)
                p_copy(p, d, True, q).start()

        @pl.when(s == n - 1)
        def _():
            @pl.loop(0, n - 1)
            def _(d):
                sendb[q][p, d] = part[p, d, :, cuts[q]].astype(jnp.bfloat16)
                p_copy(p, d, False, q).start()

    def dots(p):
        features = xg[p].astype(jnp.float32)
        sh, sl = two_parts(features * features)
        squares[s, :, pl.ds(pl.multiple_of(p * rows, 128), rows)] = matmul_nt(ones, sh) + matmul_nt(ones, sl)
        y = (features * gain).astype(jnp.bfloat16)

        @pl.loop(0, n)
        def _(d):
            part[p, d] = matmul(y, wv[d])

    def chain(p, q):
        @pl.when((s > 0) & (s < n - 1))
        def _():
            @pl.loop(0, n - 1)
            def _(i):
                d = n - 1 - i

                @pl.when(d > s)
                def _():
                    p_copy(p, d, True, q).wait_recv()
                    sendb[q][p, d] = (
                        part[p, d, :, cuts[q]] + from_low[q][p, d].astype(jnp.float32)
                    ).astype(jnp.bfloat16)
                    p_copy(p, d, True, q).start()

                @pl.when(i < s)
                def _():
                    p_copy(p, i, False, q).wait_recv()
                    sendb[q][p, i] = (
                        part[p, i, :, cuts[q]] + from_high[q][p, i].astype(jnp.float32)
                    ).astype(jnp.bfloat16)
                    p_copy(p, i, False, q).start()

    def total(p, q):
        @pl.when(s > 0)
        def _():
            p_copy(p, s, True, q).wait_recv()
            part[p, s, :, cuts[q]] += from_low[q][p, s].astype(jnp.float32)

        @pl.when(s < n - 1)
        def _():
            p_copy(p, s, False, q).wait_recv()
            part[p, s, :, cuts[q]] += from_high[q][p, s].astype(jnp.float32)

    order = (t, sib, far, far_sib)
    dots(t)
    first(t, 0)
    for h in range(chunks):
        slot_copy(far, 1, far, h).wait_recv()
        slot_copy(far, 3, sib, h).start()
    for h in range(chunks):
        slot_copy(sib, 2, sib, h).wait_recv()
    dots(sib)
    first(sib, 0)
    dots(far)
    first(far, 0)
    chain(t, 0)
    for h in range(chunks):
        slot_copy(far_sib, 3, sib, h).wait_recv()
    dots(far_sib)
    first(far_sib, 0)

    q_copies = []
    for k in range(1, n):
        q_copy = remote(squares.at[s], squares.at[s], q_send.at[k], q_recv.at[s], lax.rem(s + k, n), t)
        q_copy.start()
        q_copies.append(q_copy)
    for p in order:
        first(p, 1)
    filter_load.wait()
    fh, fl = two_parts(filter_ref[...])
    loads[3 * n].wait()
    loads[3 * n + 1].wait()
    spectrum[...] = matmul_nt(ah[...], fh) + matmul_nt(ah[...], fl) + matmul_nt(al[...], fh)

    for p in order[1:]:
        chain(p, 0)

    for k in range(1, n):
        other = lax.rem(s + k, n)
        remote(squares.at[other], squares.at[other], q_send.at[k], q_recv.at[other], other, t).wait_recv()
    all_squares = squares[0] + squares[1] + squares[2] + squares[3]
    scale = lax.rsqrt(all_squares * (1.0 / (n * width)) + EPSILON)
    scale = jnp.transpose(jnp.broadcast_to(scale[0:1], (ch, length)))
    taps_load.wait()
    for p in order:
        total(p, 0)

    row = lax.broadcasted_iota(jnp.int32, (length, ch), 0)

    def filtered(j):
        at = (j + 2) % 3 * ch
        projected = jnp.concatenate([part[p, s, :, at:at + ch] for p in range(n)], axis=0) * scale
        taps = [taps_ref[j, o:o + 1, :] for o in range(3)]
        value = taps[0] * projected
        for o in range(1, 3):
            value = value + taps[o] * jnp.where(row >= o, pltpu.roll(projected, o, 0), 0.0)
        return value

    kh, kl = two_parts(filtered(1) * filtered(2))
    chain(order[0], 1)
    both = matmul(ah[...], jnp.concatenate([kh, kl], axis=1))
    signal = both[:, :ch] + both[:, ch:] + matmul(al[...], kh)
    chain(order[1], 1)
    a, b = signal[:length], signal[length:]
    c, e = spectrum[:length], spectrum[length:]
    yh, yl = two_parts(jnp.concatenate([a * c - b * e, a * e + b * c], axis=0))
    for load in loads[3 * n + 2:3 * n + 5]:
        load.wait()
    chain(order[2], 1)
    both = matmul(bh[...], jnp.concatenate([yh, yl], axis=1))
    conv = (both[:, :ch] + both[:, ch:] + matmul(bl[...], yh)) * (1.0 / length)
    chain(order[3], 1)
    for p in order:
        total(p, 1)
    query = filtered(0)

    gathered[s] = (query * conv).astype(jnp.bfloat16)

    def g_copy(i, up):
        sems = g_right if up else g_left
        return remote(
            gathered.at[i], gathered.at[i], sems.at[i], g_recv.at[i],
            s + 1 if up else s - 1, t,
        )

    @pl.when(s < n - 1)
    def _():
        g_copy(s, True).start()

    @pl.when(s > 0)
    def _():
        g_copy(s, False).start()

    for k in range(1, n):
        @pl.when(s - k >= 0)
        def _():
            g_copy(s - k, True).wait_recv()

            @pl.when(s < n - 1)
            def _():
                g_copy(s - k, True).start()

        @pl.when(s + k < n)
        def _():
            g_copy(s + k, False).wait_recv()

            @pl.when(s > 0)
            def _():
                g_copy(s + k, False).start()

    def term(p):
        at = pl.ds(pl.multiple_of(p * rows, 128), rows)
        return matmul_nt(jnp.concatenate([gathered[i, at] for i in range(n)], axis=1), wo[...])

    def hop(which, target, to_s, to_t, h):
        return remote(
            terms.at[which, piece(h)], target.at[piece(h)], t_send.at[which, h], t_recv.at[which, h], to_s, to_t
        )

    def far_out(h):
        return hop(0, sibling_in.at[0], s, sib, h)

    def own_out(h):
        return hop(1, sibling_in.at[1], s, sib, h)

    def cross(h):
        return hop(2, cross_in, s, far, h)

    def final(h):
        return hop(3, final_in, t, s, h)

    terms[0] = term(far_sib).astype(jnp.bfloat16)
    for h in range(chunks):
        far_out(h).start()
    terms_acc[...] = term(far)
    for h in range(chunks):
        far_out(h).wait_recv()
        terms[2, piece(h)] = (
            terms_acc[piece(h)] + sibling_in[0, piece(h)].astype(jnp.float32)
        ).astype(jnp.bfloat16)
        cross(h).start()
    terms[1] = term(sib).astype(jnp.bfloat16)
    for h in range(chunks):
        own_out(h).start()
    terms_acc[...] = term(t)
    for h in range(chunks):
        own_out(h).wait_recv()
        terms_acc[piece(h)] += sibling_in[1, piece(h)].astype(jnp.float32)
    for h in range(chunks):
        cross(h).wait_recv()
        value = terms_acc[piece(h)] + cross_in[piece(h)].astype(jnp.float32)

        @pl.when(s != t)
        def _():
            terms[3, piece(h)] = value.astype(jnp.bfloat16)
            final(h).start()

        @pl.when(s == t)
        def _():
            out_ref[piece(h)] = x_ref[piece(h)] + value

    @pl.when(s != t)
    def _():
        for h in range(chunks):
            final(h).wait_recv()
            out_ref[piece(h)] = x_ref[piece(h)] + final_in[piece(h)].astype(jnp.float32)
        for h in range(chunks):
            swap(h, s).wait_send()
            final(h).wait_send()

    for h in range(chunks):
        for copy in (
            slot_copy(t, 1, far, h), slot_copy(t, 2, sib, h), slot_copy(far, 3, sib, h),
            far_out(h), own_out(h), cross(h),
        ):
            copy.wait_send()
    for copy in q_copies:
        copy.wait_send()
    for p in order:
        for q in range(2):
            @pl.loop(0, n)
            def _(d):
                @pl.when(d > s)
                def _():
                    p_copy(p, d, True, q).wait_send()

                @pl.when(d < s)
                def _():
                    p_copy(p, d, False, q).wait_send()

    @pl.loop(0, n)
    def _(i):
        @pl.when((i <= s) & (s < n - 1))
        def _():
            g_copy(i, True).wait_send()

        @pl.when((i >= s) & (s > 0))
        def _():
            g_copy(i, False).wait_send()


def kernel_shards(residual_in, norm_gain, in_weight, short_taps, long_filter, out_weight):
    n = 4
    rows, width = residual_in.shape
    ch, length = long_filter.shape
    tables = [jnp.asarray(table) for table in transform_tables(length)]
    vmem, hbm = pl.BlockSpec(memory_space=pltpu.VMEM), pl.BlockSpec(memory_space=pl.ANY)
    dma = pltpu.SemaphoreType.DMA
    bf16, f32 = jnp.bfloat16, jnp.float32
    return pl.pallas_call(
        block_kernel,
        out_shape=jax.ShapeDtypeStruct((rows, width), f32),
        in_specs=[hbm] * 10,
        out_specs=vmem,
        scratch_shapes=[
            pltpu.VMEM((rows, width), f32),
            pltpu.VMEM((1, width), f32),
            pltpu.VMEM(short_taps.shape[:2] + (ch,), f32),
            pltpu.VMEM((ch, length), f32),
            pltpu.VMEM((n, width, 3 * ch), bf16),
            pltpu.VMEM(out_weight.shape, bf16),
            pltpu.VMEM((2 * length, length), bf16),
            pltpu.VMEM((2 * length, length), bf16),
            pltpu.VMEM((length, 2 * length), bf16),
            pltpu.VMEM((length, 2 * length), bf16),
            pltpu.VMEM((rows, width), bf16),
            pltpu.VMEM((n, rows, width), bf16),
            pltpu.VMEM((n, n, rows, 3 * ch), f32),
            pltpu.VMEM((n, n, rows, 2 * ch), bf16),
            pltpu.VMEM((n, n, rows, ch), bf16),
            pltpu.VMEM((n, n, rows, 2 * ch), bf16),
            pltpu.VMEM((n, n, rows, ch), bf16),
            pltpu.VMEM((n, n, rows, 2 * ch), bf16),
            pltpu.VMEM((n, n, rows, ch), bf16),
            pltpu.VMEM((n, 8, length), f32),
            pltpu.VMEM((2 * length, ch), f32),
            pltpu.VMEM((n, length, ch), bf16),
            pltpu.VMEM((n, rows, width), bf16),
            pltpu.VMEM((rows, width), f32),
            pltpu.VMEM((2, rows, width), bf16),
            pltpu.VMEM((rows, width), bf16),
            pltpu.VMEM((rows, width), bf16),
            dma((3 * n + 9,)), dma((n, n)), dma((n, n)), dma((2, n, n)), dma((2, n, n)), dma((2, n, n)),
            dma((n,)), dma((n,)), dma((n,)), dma((n,)), dma((n,)), dma((n, n)), dma((n, n)),
        ],
        compiler_params=pltpu.CompilerParams(
            collective_id=0, has_side_effects=True, vmem_limit_bytes=60 * 1024 * 1024
        ),
    )(residual_in, norm_gain[None], in_weight, short_taps, long_filter, out_weight, *tables)


def solution(mesh):
    square = mesh.shape["seq"] == 4 and mesh.shape["tensor"] == 4
    return jax.shard_map(
        kernel_shards if square else shards,
        mesh=mesh,
        in_specs=(
            P(("groups", "seq"), "tensor"),
            P(),
            P(None, "seq", "tensor"),
            P(None, None, "tensor"),
            P(("tensor", "seq"), None),
            P("seq", "tensor"),
        ),
        out_specs=P(("groups", "seq"), "tensor"),
        check_vma=False,
    )
```

```python
import math

import jax
import jax.numpy as jnp
import ml_dtypes
import numpy as np
from jax import lax
from jax.experimental import pallas as pl
from jax.experimental.pallas import tpu as pltpu
from jax.sharding import PartitionSpec as P

EPSILON = 1e-05


def shifted(value, axis, by):
    length = lax.axis_size(axis)
    pairs = [(i, i + by) for i in range(length) if 0 <= i + by < length]
    return lax.ppermute(value, axis, pairs)


def exact_product(form, left, right):
    return jnp.einsum(form, left, right, precision=lax.Precision.HIGHEST)


def angle_tables(modulus, count_a, count_b):
    index_a = jnp.arange(count_a, dtype=jnp.int32)[:, None]
    index_b = jnp.arange(count_b, dtype=jnp.int32)[None, :]
    theta = (index_a * index_b % modulus).astype(jnp.float32) * (2.0 * math.pi / modulus)
    return (jnp.cos(theta), jnp.sin(theta))


def split_length(full_length):
    low_factor = 1
    while full_length % (4 * low_factor) == 0 and 4 * low_factor * low_factor <= full_length:
        low_factor = low_factor * 2
    return (low_factor, full_length // low_factor)


def forward_spectrum(signal, low_factor, high_factor, all_tables):
    cos_high, sin_high, cos_twist, sin_twist, cos_low, sin_low = all_tables
    channel_count = signal.shape[0]
    blocks = signal.reshape(channel_count, high_factor // 2, low_factor)
    real_a = exact_product("cmp,mk->cpk", blocks, cos_high)
    imag_a = -exact_product("cmp,mk->cpk", blocks, sin_high)
    real_b = real_a * cos_twist + imag_a * sin_twist
    imag_b = imag_a * cos_twist - real_a * sin_twist
    real_x = exact_product("cpk,pj->cjk", real_b, cos_low) + exact_product(
        "cpk,pj->cjk", imag_b, sin_low
    )
    imag_x = exact_product("cpk,pj->cjk", imag_b, cos_low) - exact_product(
        "cpk,pj->cjk", real_b, sin_low
    )
    return (real_x, imag_x)


def inverse_signal(real_x, imag_x, low_factor, high_factor, all_tables):
    cos_high, sin_high, cos_twist, sin_twist, cos_low, sin_low = all_tables
    channel_count = real_x.shape[0]
    real_b = exact_product("cjk,pj->cpk", real_x, cos_low) - exact_product(
        "cjk,pj->cpk", imag_x, sin_low
    )
    imag_b = exact_product("cjk,pj->cpk", real_x, sin_low) + exact_product(
        "cjk,pj->cpk", imag_x, cos_low
    )
    real_c = real_b * cos_twist - imag_b * sin_twist
    imag_c = real_b * sin_twist + imag_b * cos_twist
    result = exact_product("cpk,mk->cmp", real_c, cos_high) - exact_product(
        "cpk,mk->cmp", imag_c, sin_high
    )
    full_length = low_factor * high_factor
    return (result / full_length).reshape(channel_count, full_length // 2)


def shards(residual_in, norm_gain, in_weight, short_taps, long_filter, out_weight):
    row_count, local_width = residual_in.shape
    full_rows = lax.all_gather(
        residual_in.astype(jnp.bfloat16), "tensor", axis=1, tiled=True
    ).astype(residual_in.dtype)
    mean_sq = jnp.mean(full_rows * full_rows, axis=1, keepdims=True)
    normed = (full_rows * lax.rsqrt(mean_sq + EPSILON) * norm_gain).astype(jnp.bfloat16)
    projected = jnp.einsum(
        "rd,sdc->scr",
        normed,
        lax.all_gather(in_weight, "seq", axis=1, tiled=True),
        preferred_element_type=jnp.float32,
    )
    reach = short_taps.shape[1] - 1
    earlier = shifted(projected[:, :, row_count - reach :], "seq", 1)
    extended = jnp.concatenate([earlier, projected], axis=2)
    mixed = short_taps[:, 0, :, None] * projected
    for offset in range(1, reach + 1):
        mixed = (
            mixed
            + short_taps[:, offset, :, None]
            * extended[:, :, reach - offset : reach - offset + row_count]
        )
    query = mixed[0]
    product_kv = mixed[1] * mixed[2]
    by_channel = lax.all_to_all(
        product_kv.astype(jnp.bfloat16), "seq", split_axis=0, concat_axis=1, tiled=True
    ).astype(product_kv.dtype)
    full_length = 2 * by_channel.shape[1]
    low_factor, high_factor = split_length(full_length)
    cos_high, sin_high = angle_tables(high_factor, high_factor // 2, high_factor)
    cos_twist, sin_twist = angle_tables(full_length, low_factor, high_factor)
    cos_low, sin_low = angle_tables(low_factor, low_factor, low_factor)
    all_tables = (cos_high, sin_high, cos_twist, sin_twist, cos_low, sin_low)
    signal_real, signal_imag = forward_spectrum(by_channel, low_factor, high_factor, all_tables)
    filter_real, filter_imag = forward_spectrum(long_filter, low_factor, high_factor, all_tables)
    conv = inverse_signal(
        signal_real * filter_real - signal_imag * filter_imag,
        signal_real * filter_imag + signal_imag * filter_real,
        low_factor,
        high_factor,
        all_tables,
    )
    returned = lax.all_to_all(
        conv.astype(jnp.bfloat16), "seq", split_axis=1, concat_axis=0, tiled=True
    ).astype(conv.dtype)
    gated = (query * returned).astype(jnp.bfloat16)
    terms = jnp.einsum(
        "cr,nc->rn",
        gated,
        lax.all_gather(out_weight, "seq", axis=0, tiled=True),
        preferred_element_type=jnp.float32,
    )
    summed = lax.psum_scatter(
        terms.astype(jnp.bfloat16), "tensor", scatter_dimension=1, tiled=True
    ).astype(jnp.float32)
    return residual_in + summed


MESH = pl.DeviceIdType.MESH


def transform_tables(length):
    index = np.arange(length)
    turns = ((2 * index[:, None] + 1) * index[None, :]) % (4 * length)
    theta = turns.astype(np.float64) * (math.pi / (2 * length))
    table = np.concatenate([np.cos(theta), np.sin(theta)], axis=0).astype(np.float32)
    high = table.astype(ml_dtypes.bfloat16)
    low = (table - high.astype(np.float32)).astype(ml_dtypes.bfloat16)
    return (high, low, np.ascontiguousarray(high.T), np.ascontiguousarray(low.T))


def two_parts(value):
    high = value.astype(jnp.bfloat16)
    low = (value - high.astype(jnp.float32)).astype(jnp.bfloat16)
    return (high, low)


def matmul(left, right):
    return jnp.dot(left, right, preferred_element_type=jnp.float32)


def matmul_nt(left, right):
    return lax.dot_general(left, right, (((1,), (1,)), ((), ())), preferred_element_type=jnp.float32)


def block_kernel(
    x_hbm, gain_hbm, w_hbm, taps_hbm, filter_hbm, wo_hbm, ah_hbm, al_hbm, bh_hbm, bl_hbm,
    out_ref,
    x_ref, gain_ref, taps_ref, filter_ref, wv, wo, ah, al, bh, bl, xb, xg, part, sendb, inbox, squares, spectrum,
    gathered, terms, terms_acc, sibling_in, cross_in, final_in,
    load_sem, x_send, x_recv, p_send, p_recv, q_send, q_recv,
    g_right, g_left, g_recv, t_send, t_recv,
):
    s = lax.axis_index("seq")
    t = lax.axis_index("tensor")
    n = 4
    rows, width = x_ref.shape
    ch = filter_ref.shape[0]
    length = filter_ref.shape[1]
    sib = t + 1 - 2 * lax.rem(t, 2)
    far = lax.rem(t + 2, n)
    far_sib = lax.rem(sib + 2, n)

    chunks = 4
    step = rows // chunks

    def lanes(i):
        return pl.ds(pl.multiple_of(i * ch, 128), ch)

    loads = []
    for d in range(n):
        for j in range(3):
            loads.append(pltpu.make_async_copy(
                w_hbm.at[(j + 1) % 3, :, pl.ds(d * ch, ch)],
                wv.at[d, :, pl.ds(j * ch, ch)],
                load_sem.at[d * 3 + j],
            ))
    for i, (source, target) in enumerate((
        (ah_hbm, ah), (al_hbm, al), (wo_hbm, wo), (bh_hbm, bh), (bl_hbm, bl),
        (x_hbm, x_ref), (filter_hbm, filter_ref), (taps_hbm.at[:, :, lanes(s)], taps_ref),
        (gain_hbm.at[:, pl.ds(pl.multiple_of(s * width, 128), width)], gain_ref),
    )):
        loads.append(pltpu.make_async_copy(source, target, load_sem.at[3 * n + i]))
    x_load, filter_load, taps_load, gain_load = loads[3 * n + 5:]
    x_load.start()

    barrier = pltpu.get_barrier_semaphore()
    for k in range(1, n):
        pl.semaphore_signal(barrier, inc=1, device_id={"seq": lax.rem(s + k, n), "tensor": t}, device_id_type=MESH)
        pl.semaphore_signal(barrier, inc=1, device_id={"seq": s, "tensor": lax.rem(t + k, n)}, device_id_type=MESH)

    @pl.when(s != t)
    def _():
        pl.semaphore_signal(barrier, inc=1, device_id={"seq": t, "tensor": s}, device_id_type=MESH)

    x_load.wait()
    xb[...] = x_ref[...].astype(jnp.bfloat16)

    @pl.when(s != t)
    def _():
        pl.semaphore_wait(barrier, 2 * n - 1)

    @pl.when(s == t)
    def _():
        pl.semaphore_wait(barrier, 2 * n - 2)

    def remote(source, target, send, recv, to_s, to_t):
        return pltpu.make_async_remote_copy(
            src_ref=source, dst_ref=target, send_sem=send, recv_sem=recv,
            device_id={"seq": to_s, "tensor": to_t}, device_id_type=MESH,
        )

    def piece(h):
        return pl.ds(h * step, step)

    def swap(h, slot):
        return remote(
            xb.at[piece(h)], xg.at[slot, piece(h)], x_send.at[0, h], x_recv.at[slot, h], t, s
        )

    @pl.when(s != t)
    def _():
        for h in range(chunks):
            swap(h, s).start()

    gain_load.start()
    for load in loads[:3 * n] + [filter_load] + loads[3 * n:3 * n + 2] + [taps_load] + loads[3 * n + 2:3 * n + 5]:
        load.start()

    def slot_copy(slot, which, to_t, h):
        return remote(
            xg.at[slot, piece(h)], xg.at[slot, piece(h)], x_send.at[which, h], x_recv.at[slot, h], s, to_t
        )

    @pl.when(s == t)
    def _():
        xg[t] = xb[...]

    for h in range(chunks):
        @pl.when(s != t)
        def _():
            swap(h, t).wait_recv()

        slot_copy(t, 1, far, h).start()
        slot_copy(t, 2, sib, h).start()

    for load in loads[: 3 * n]:
        load.wait()
    gain_load.wait()
    gain = gain_ref[...]
    ones = jnp.ones((8, width), jnp.bfloat16)

    def p_copy(p, d, slot):
        return remote(sendb.at[p, d], inbox.at[p, slot], p_send.at[p, d], p_recv.at[p, slot], d, t)

    others = [lax.rem(s + k, n) for k in (2, 1, 3)]

    def dots(p):
        features = xg[p].astype(jnp.float32)
        sh, sl = two_parts(features * features)
        squares[s, :, pl.ds(pl.multiple_of(p * rows, 128), rows)] = matmul_nt(ones, sh) + matmul_nt(ones, sl)
        y = (features * gain).astype(jnp.bfloat16)

        @pl.loop(0, n)
        def _(d):
            part[p, d] = matmul(y, wv[d])

        for d in others:
            sendb[p, d] = part[p, d].astype(jnp.bfloat16)
            p_copy(p, d, s).start()

    def total(p):
        for k in others:
            p_copy(p, k, k).wait_recv()
        value = part[p, s]
        for k in others:
            value = value + inbox[p, k].astype(jnp.float32)
        part[p, s] = value

    order = (t, sib, far, far_sib)
    dots(t)
    for h in range(chunks):
        slot_copy(far, 1, far, h).wait_recv()
        slot_copy(far, 3, sib, h).start()
    for h in range(chunks):
        slot_copy(sib, 2, sib, h).wait_recv()
    dots(sib)
    dots(far)
    for h in range(chunks):
        slot_copy(far_sib, 3, sib, h).wait_recv()
    dots(far_sib)

    q_copies = []
    for k in range(1, n):
        q_copy = remote(squares.at[s], squares.at[s], q_send.at[k], q_recv.at[s], lax.rem(s + k, n), t)
        q_copy.start()
        q_copies.append(q_copy)
    filter_load.wait()
    fh, fl = two_parts(filter_ref[...])
    loads[3 * n].wait()
    loads[3 * n + 1].wait()
    spectrum[...] = matmul_nt(ah[...], fh) + matmul_nt(ah[...], fl) + matmul_nt(al[...], fh)


    for k in range(1, n):
        other = lax.rem(s + k, n)
        remote(squares.at[other], squares.at[other], q_send.at[k], q_recv.at[other], other, t).wait_recv()
    all_squares = squares[0] + squares[1] + squares[2] + squares[3]
    scale = lax.rsqrt(all_squares * (1.0 / (n * width)) + EPSILON)
    scale = jnp.transpose(jnp.broadcast_to(scale[0:1], (ch, length)))
    taps_load.wait()
    for p in order:
        total(p)

    row = lax.broadcasted_iota(jnp.int32, (length, ch), 0)

    def filtered(j):
        at = (j + 2) % 3 * ch
        projected = jnp.concatenate([part[p, s, :, at:at + ch] for p in range(n)], axis=0) * scale
        taps = [taps_ref[j, o:o + 1, :] for o in range(3)]
        value = taps[0] * projected
        for o in range(1, 3):
            value = value + taps[o] * jnp.where(row >= o, pltpu.roll(projected, o, 0), 0.0)
        return value

    kh, kl = two_parts(filtered(1) * filtered(2))
    both = matmul(ah[...], jnp.concatenate([kh, kl], axis=1))
    signal = both[:, :ch] + both[:, ch:] + matmul(al[...], kh)
    a, b = signal[:length], signal[length:]
    c, e = spectrum[:length], spectrum[length:]
    yh, yl = two_parts(jnp.concatenate([a * c - b * e, a * e + b * c], axis=0))
    for load in loads[3 * n + 2:3 * n + 5]:
        load.wait()
    both = matmul(bh[...], jnp.concatenate([yh, yl], axis=1))
    conv = (both[:, :ch] + both[:, ch:] + matmul(bl[...], yh)) * (1.0 / length)
    query = filtered(0)

    gathered[s] = (query * conv).astype(jnp.bfloat16)

    def g_copy(i, up):
        sems = g_right if up else g_left
        return remote(
            gathered.at[i], gathered.at[i], sems.at[i], g_recv.at[i],
            s + 1 if up else s - 1, t,
        )

    @pl.when(s < n - 1)
    def _():
        g_copy(s, True).start()

    @pl.when(s > 0)
    def _():
        g_copy(s, False).start()

    for k in range(1, n):
        @pl.when(s - k >= 0)
        def _():
            g_copy(s - k, True).wait_recv()

            @pl.when(s < n - 1)
            def _():
                g_copy(s - k, True).start()

        @pl.when(s + k < n)
        def _():
            g_copy(s + k, False).wait_recv()

            @pl.when(s > 0)
            def _():
                g_copy(s + k, False).start()

    def term(p):
        at = pl.ds(pl.multiple_of(p * rows, 128), rows)
        return matmul_nt(jnp.concatenate([gathered[i, at] for i in range(n)], axis=1), wo[...])

    def hop(which, target, to_s, to_t, h):
        return remote(
            terms.at[which, piece(h)], target.at[piece(h)], t_send.at[which, h], t_recv.at[which, h], to_s, to_t
        )

    def far_out(h):
        return hop(0, sibling_in.at[0], s, sib, h)

    def own_out(h):
        return hop(1, sibling_in.at[1], s, sib, h)

    def cross(h):
        return hop(2, cross_in, s, far, h)

    def final(h):
        return hop(3, final_in, t, s, h)

    terms[0] = term(far_sib).astype(jnp.bfloat16)
    for h in range(chunks):
        far_out(h).start()
    terms_acc[...] = term(far)
    for h in range(chunks):
        far_out(h).wait_recv()
        terms[2, piece(h)] = (
            terms_acc[piece(h)] + sibling_in[0, piece(h)].astype(jnp.float32)
        ).astype(jnp.bfloat16)
        cross(h).start()
    terms[1] = term(sib).astype(jnp.bfloat16)
    for h in range(chunks):
        own_out(h).start()
    terms_acc[...] = term(t)
    for h in range(chunks):
        own_out(h).wait_recv()
        terms_acc[piece(h)] += sibling_in[1, piece(h)].astype(jnp.float32)
    for h in range(chunks):
        cross(h).wait_recv()
        value = terms_acc[piece(h)] + cross_in[piece(h)].astype(jnp.float32)

        @pl.when(s != t)
        def _():
            terms[3, piece(h)] = value.astype(jnp.bfloat16)
            final(h).start()

        @pl.when(s == t)
        def _():
            out_ref[piece(h)] = x_ref[piece(h)] + value

    @pl.when(s != t)
    def _():
        for h in range(chunks):
            final(h).wait_recv()
            out_ref[piece(h)] = x_ref[piece(h)] + final_in[piece(h)].astype(jnp.float32)
        for h in range(chunks):
            swap(h, s).wait_send()
            final(h).wait_send()

    for h in range(chunks):
        for copy in (
            slot_copy(t, 1, far, h), slot_copy(t, 2, sib, h), slot_copy(far, 3, sib, h),
            far_out(h), own_out(h), cross(h),
        ):
            copy.wait_send()
    for copy in q_copies:
        copy.wait_send()
    for p in order:
        for d in others:
            p_copy(p, d, s).wait_send()

    @pl.loop(0, n)
    def _(i):
        @pl.when((i <= s) & (s < n - 1))
        def _():
            g_copy(i, True).wait_send()

        @pl.when((i >= s) & (s > 0))
        def _():
            g_copy(i, False).wait_send()


def kernel_shards(residual_in, norm_gain, in_weight, short_taps, long_filter, out_weight):
    n = 4
    rows, width = residual_in.shape
    ch, length = long_filter.shape
    tables = [jnp.asarray(table) for table in transform_tables(length)]
    vmem, hbm = pl.BlockSpec(memory_space=pltpu.VMEM), pl.BlockSpec(memory_space=pl.ANY)
    dma = pltpu.SemaphoreType.DMA
    bf16, f32 = jnp.bfloat16, jnp.float32
    return pl.pallas_call(
        block_kernel,
        out_shape=jax.ShapeDtypeStruct((rows, width), f32),
        in_specs=[hbm] * 10,
        out_specs=vmem,
        scratch_shapes=[
            pltpu.VMEM((rows, width), f32),
            pltpu.VMEM((1, width), f32),
            pltpu.VMEM(short_taps.shape[:2] + (ch,), f32),
            pltpu.VMEM((ch, length), f32),
            pltpu.VMEM((n, width, 3 * ch), bf16),
            pltpu.VMEM(out_weight.shape, bf16),
            pltpu.VMEM((2 * length, length), bf16),
            pltpu.VMEM((2 * length, length), bf16),
            pltpu.VMEM((length, 2 * length), bf16),
            pltpu.VMEM((length, 2 * length), bf16),
            pltpu.VMEM((rows, width), bf16),
            pltpu.VMEM((n, rows, width), bf16),
            pltpu.VMEM((n, n, rows, 3 * ch), f32),
            pltpu.VMEM((n, n, rows, 3 * ch), bf16),
            pltpu.VMEM((n, n, rows, 3 * ch), bf16),
            pltpu.VMEM((n, 8, length), f32),
            pltpu.VMEM((2 * length, ch), f32),
            pltpu.VMEM((n, length, ch), bf16),
            pltpu.VMEM((n, rows, width), bf16),
            pltpu.VMEM((rows, width), f32),
            pltpu.VMEM((2, rows, width), bf16),
            pltpu.VMEM((rows, width), bf16),
            pltpu.VMEM((rows, width), bf16),
            dma((3 * n + 9,)), dma((n, n)), dma((n, n)), dma((n, n)), dma((n, n)),
            dma((n,)), dma((n,)), dma((n,)), dma((n,)), dma((n,)), dma((n, n)), dma((n, n)),
        ],
        compiler_params=pltpu.CompilerParams(
            collective_id=0, has_side_effects=True, vmem_limit_bytes=60 * 1024 * 1024
        ),
    )(residual_in, norm_gain[None], in_weight, short_taps, long_filter, out_weight, *tables)


def solution(mesh):
    square = mesh.shape["seq"] == 4 and mesh.shape["tensor"] == 4
    return jax.shard_map(
        kernel_shards if square else shards,
        mesh=mesh,
        in_specs=(
            P(("groups", "seq"), "tensor"),
            P(),
            P(None, "seq", "tensor"),
            P(None, None, "tensor"),
            P(("tensor", "seq"), None),
            P("seq", "tensor"),
        ),
        out_specs=P(("groups", "seq"), "tensor"),
        check_vma=False,
    )
```

```python
import math

import jax
import jax.numpy as jnp
import ml_dtypes
import numpy as np
from jax import lax
from jax.experimental import pallas as pl
from jax.experimental.pallas import tpu as pltpu
from jax.sharding import PartitionSpec as P

EPSILON = 1e-05


def shifted(value, axis, by):
    length = lax.axis_size(axis)
    pairs = [(i, i + by) for i in range(length) if 0 <= i + by < length]
    return lax.ppermute(value, axis, pairs)


def exact_product(form, left, right):
    return jnp.einsum(form, left, right, precision=lax.Precision.HIGHEST)


def angle_tables(modulus, count_a, count_b):
    index_a = jnp.arange(count_a, dtype=jnp.int32)[:, None]
    index_b = jnp.arange(count_b, dtype=jnp.int32)[None, :]
    theta = (index_a * index_b % modulus).astype(jnp.float32) * (2.0 * math.pi / modulus)
    return (jnp.cos(theta), jnp.sin(theta))


def split_length(full_length):
    low_factor = 1
    while full_length % (4 * low_factor) == 0 and 4 * low_factor * low_factor <= full_length:
        low_factor = low_factor * 2
    return (low_factor, full_length // low_factor)


def forward_spectrum(signal, low_factor, high_factor, all_tables):
    cos_high, sin_high, cos_twist, sin_twist, cos_low, sin_low = all_tables
    channel_count = signal.shape[0]
    blocks = signal.reshape(channel_count, high_factor // 2, low_factor)
    real_a = exact_product("cmp,mk->cpk", blocks, cos_high)
    imag_a = -exact_product("cmp,mk->cpk", blocks, sin_high)
    real_b = real_a * cos_twist + imag_a * sin_twist
    imag_b = imag_a * cos_twist - real_a * sin_twist
    real_x = exact_product("cpk,pj->cjk", real_b, cos_low) + exact_product(
        "cpk,pj->cjk", imag_b, sin_low
    )
    imag_x = exact_product("cpk,pj->cjk", imag_b, cos_low) - exact_product(
        "cpk,pj->cjk", real_b, sin_low
    )
    return (real_x, imag_x)


def inverse_signal(real_x, imag_x, low_factor, high_factor, all_tables):
    cos_high, sin_high, cos_twist, sin_twist, cos_low, sin_low = all_tables
    channel_count = real_x.shape[0]
    real_b = exact_product("cjk,pj->cpk", real_x, cos_low) - exact_product(
        "cjk,pj->cpk", imag_x, sin_low
    )
    imag_b = exact_product("cjk,pj->cpk", real_x, sin_low) + exact_product(
        "cjk,pj->cpk", imag_x, cos_low
    )
    real_c = real_b * cos_twist - imag_b * sin_twist
    imag_c = real_b * sin_twist + imag_b * cos_twist
    result = exact_product("cpk,mk->cmp", real_c, cos_high) - exact_product(
        "cpk,mk->cmp", imag_c, sin_high
    )
    full_length = low_factor * high_factor
    return (result / full_length).reshape(channel_count, full_length // 2)


def shards(residual_in, norm_gain, in_weight, short_taps, long_filter, out_weight):
    row_count, local_width = residual_in.shape
    full_rows = lax.all_gather(
        residual_in.astype(jnp.bfloat16), "tensor", axis=1, tiled=True
    ).astype(residual_in.dtype)
    mean_sq = jnp.mean(full_rows * full_rows, axis=1, keepdims=True)
    normed = (full_rows * lax.rsqrt(mean_sq + EPSILON) * norm_gain).astype(jnp.bfloat16)
    projected = jnp.einsum(
        "rd,sdc->scr",
        normed,
        lax.all_gather(in_weight, "seq", axis=1, tiled=True),
        preferred_element_type=jnp.float32,
    )
    reach = short_taps.shape[1] - 1
    earlier = shifted(projected[:, :, row_count - reach :], "seq", 1)
    extended = jnp.concatenate([earlier, projected], axis=2)
    mixed = short_taps[:, 0, :, None] * projected
    for offset in range(1, reach + 1):
        mixed = (
            mixed
            + short_taps[:, offset, :, None]
            * extended[:, :, reach - offset : reach - offset + row_count]
        )
    query = mixed[0]
    product_kv = mixed[1] * mixed[2]
    by_channel = lax.all_to_all(
        product_kv.astype(jnp.bfloat16), "seq", split_axis=0, concat_axis=1, tiled=True
    ).astype(product_kv.dtype)
    full_length = 2 * by_channel.shape[1]
    low_factor, high_factor = split_length(full_length)
    cos_high, sin_high = angle_tables(high_factor, high_factor // 2, high_factor)
    cos_twist, sin_twist = angle_tables(full_length, low_factor, high_factor)
    cos_low, sin_low = angle_tables(low_factor, low_factor, low_factor)
    all_tables = (cos_high, sin_high, cos_twist, sin_twist, cos_low, sin_low)
    signal_real, signal_imag = forward_spectrum(by_channel, low_factor, high_factor, all_tables)
    filter_real, filter_imag = forward_spectrum(long_filter, low_factor, high_factor, all_tables)
    conv = inverse_signal(
        signal_real * filter_real - signal_imag * filter_imag,
        signal_real * filter_imag + signal_imag * filter_real,
        low_factor,
        high_factor,
        all_tables,
    )
    returned = lax.all_to_all(
        conv.astype(jnp.bfloat16), "seq", split_axis=1, concat_axis=0, tiled=True
    ).astype(conv.dtype)
    gated = (query * returned).astype(jnp.bfloat16)
    terms = jnp.einsum(
        "cr,nc->rn",
        gated,
        lax.all_gather(out_weight, "seq", axis=0, tiled=True),
        preferred_element_type=jnp.float32,
    )
    summed = lax.psum_scatter(
        terms.astype(jnp.bfloat16), "tensor", scatter_dimension=1, tiled=True
    ).astype(jnp.float32)
    return residual_in + summed


MESH = pl.DeviceIdType.MESH


def transform_tables(length):
    index = np.arange(length)
    turns = ((2 * index[:, None] + 1) * index[None, :]) % (4 * length)
    theta = turns.astype(np.float64) * (math.pi / (2 * length))
    table = np.concatenate([np.cos(theta), np.sin(theta)], axis=0).astype(np.float32)
    high = table.astype(ml_dtypes.bfloat16)
    low = (table - high.astype(np.float32)).astype(ml_dtypes.bfloat16)
    return (high, low, np.ascontiguousarray(high.T), np.ascontiguousarray(low.T))


def two_parts(value):
    high = value.astype(jnp.bfloat16)
    low = (value - high.astype(jnp.float32)).astype(jnp.bfloat16)
    return (high, low)


def matmul(left, right):
    return jnp.dot(left, right, preferred_element_type=jnp.float32)


def matmul_nt(left, right):
    return lax.dot_general(left, right, (((1,), (1,)), ((), ())), preferred_element_type=jnp.float32)


def block_kernel(
    x_hbm, gain_hbm, w_hbm, taps_hbm, filter_hbm, wo_hbm, ah_hbm, al_hbm, bh_hbm, bl_hbm,
    out_ref,
    x_ref, gain_ref, taps_ref, filter_ref, wv, wo, ah, al, bh, bl, xb, xg, part, sendb, inbox, squares, spectrum, query,
    gathered, terms, terms_acc, sibling_in, cross_in, final_in,
    load_sem, x_send, x_recv, p_send, p_recv, q_send, q_recv,
    g_send, g_recv, t_send, t_recv,
):
    s = lax.axis_index("seq")
    t = lax.axis_index("tensor")
    n = 4
    rows, width = x_ref.shape
    ch = filter_ref.shape[0]
    length = filter_ref.shape[1]
    sib = t + 1 - 2 * lax.rem(t, 2)
    far = lax.rem(t + 2, n)
    far_sib = lax.rem(sib + 2, n)

    chunks = 4
    step = rows // chunks

    def lanes(i):
        return pl.ds(pl.multiple_of(i * ch, 128), ch)

    loads = []
    for d in range(n):
        for j in range(3):
            loads.append(pltpu.make_async_copy(
                w_hbm.at[(j + 1) % 3, :, pl.ds(d * ch, ch)],
                wv.at[d, :, pl.ds(j * ch, ch)],
                load_sem.at[d * 3 + j],
            ))
    for i, (source, target) in enumerate((
        (ah_hbm, ah), (al_hbm, al), (wo_hbm, wo), (bh_hbm, bh), (bl_hbm, bl),
        (x_hbm, x_ref), (filter_hbm, filter_ref), (taps_hbm.at[:, :, lanes(s)], taps_ref),
        (gain_hbm.at[:, pl.ds(pl.multiple_of(s * width, 128), width)], gain_ref),
    )):
        loads.append(pltpu.make_async_copy(source, target, load_sem.at[3 * n + i]))
    x_load, filter_load, taps_load, gain_load = loads[3 * n + 5:]
    x_load.start()

    barrier = pltpu.get_barrier_semaphore()
    for k in range(1, n):
        pl.semaphore_signal(barrier, inc=1, device_id={"seq": lax.rem(s + k, n), "tensor": t}, device_id_type=MESH)
        pl.semaphore_signal(barrier, inc=1, device_id={"seq": s, "tensor": lax.rem(t + k, n)}, device_id_type=MESH)

    @pl.when(s != t)
    def _():
        pl.semaphore_signal(barrier, inc=1, device_id={"seq": t, "tensor": s}, device_id_type=MESH)

    x_load.wait()
    xb[...] = x_ref[...].astype(jnp.bfloat16)

    @pl.when(s != t)
    def _():
        pl.semaphore_wait(barrier, 2 * n - 1)

    @pl.when(s == t)
    def _():
        pl.semaphore_wait(barrier, 2 * n - 2)

    def remote(source, target, send, recv, to_s, to_t):
        return pltpu.make_async_remote_copy(
            src_ref=source, dst_ref=target, send_sem=send, recv_sem=recv,
            device_id={"seq": to_s, "tensor": to_t}, device_id_type=MESH,
        )

    def piece(h):
        return pl.ds(h * step, step)

    def swap(h, slot):
        return remote(
            xb.at[piece(h)], xg.at[slot, piece(h)], x_send.at[0, h], x_recv.at[slot, h], t, s
        )

    @pl.when(s != t)
    def _():
        for h in range(chunks):
            swap(h, s).start()

    gain_load.start()
    for load in loads[:3 * n] + [filter_load] + loads[3 * n:3 * n + 2] + [taps_load] + loads[3 * n + 2:3 * n + 5]:
        load.start()

    def slot_copy(slot, which, to_t, h):
        return remote(
            xg.at[slot, piece(h)], xg.at[slot, piece(h)], x_send.at[which, h], x_recv.at[slot, h], s, to_t
        )

    @pl.when(s == t)
    def _():
        xg[t] = xb[...]

    for h in range(chunks):
        @pl.when(s != t)
        def _():
            swap(h, t).wait_recv()

        slot_copy(t, 1, far, h).start()
        slot_copy(t, 2, sib, h).start()

    for load in loads[: 3 * n]:
        load.wait()
    gain_load.wait()
    gain = gain_ref[...]
    ones = jnp.ones((8, width), jnp.bfloat16)

    def p_copy(p, d, slot):
        return remote(sendb.at[p, d], inbox.at[p, slot], p_send.at[p, d], p_recv.at[p, slot], d, t)

    others = [lax.rem(s + k, n) for k in (2, 1, 3)]

    def dots(p):
        features = xg[p].astype(jnp.float32)
        sh, sl = two_parts(features * features)
        squares[s, :, pl.ds(pl.multiple_of(p * rows, 128), rows)] = matmul_nt(ones, sh) + matmul_nt(ones, sl)
        y = (features * gain).astype(jnp.bfloat16)

        @pl.loop(0, n)
        def _(d):
            part[p, d] = matmul(y, wv[d])

        for d in others:
            sendb[p, d] = part[p, d].astype(jnp.bfloat16)
            p_copy(p, d, s).start()

    def total(p):
        for k in others:
            p_copy(p, k, k).wait_recv()
        value = part[p, s]
        for k in others:
            value = value + inbox[p, k].astype(jnp.float32)
        part[p, s] = value

    order = (t, sib, far, far_sib)
    dots(t)
    for h in range(chunks):
        slot_copy(far, 1, far, h).wait_recv()
        slot_copy(far, 3, sib, h).start()
    for h in range(chunks):
        slot_copy(sib, 2, sib, h).wait_recv()
    dots(sib)
    dots(far)
    for h in range(chunks):
        slot_copy(far_sib, 3, sib, h).wait_recv()
    dots(far_sib)

    q_copies = []
    for k in range(1, n):
        q_copy = remote(squares.at[s], squares.at[s], q_send.at[k], q_recv.at[s], lax.rem(s + k, n), t)
        q_copy.start()
        q_copies.append(q_copy)
    filter_load.wait()
    fh, fl = two_parts(filter_ref[...])
    loads[3 * n].wait()
    loads[3 * n + 1].wait()
    spectrum[...] = matmul_nt(ah[...], fh) + matmul_nt(ah[...], fl) + matmul_nt(al[...], fh)


    for k in range(1, n):
        other = lax.rem(s + k, n)
        remote(squares.at[other], squares.at[other], q_send.at[k], q_recv.at[other], other, t).wait_recv()
    all_squares = squares[0] + squares[1] + squares[2] + squares[3]
    scale = lax.rsqrt(all_squares * (1.0 / (n * width)) + EPSILON)
    scale = jnp.transpose(jnp.broadcast_to(scale[0:1], (ch, length)))
    taps_load.wait()
    for p in order:
        total(p)

    row = lax.broadcasted_iota(jnp.int32, (length, ch), 0)

    def filtered(j):
        at = (j + 2) % 3 * ch
        projected = jnp.concatenate([part[p, s, :, at:at + ch] for p in range(n)], axis=0) * scale
        taps = [taps_ref[j, o:o + 1, :] for o in range(3)]
        value = taps[0] * projected
        for o in range(1, 3):
            value = value + taps[o] * jnp.where(row >= o, pltpu.roll(projected, o, 0), 0.0)
        return value

    kh, kl = two_parts(filtered(1) * filtered(2))
    both = matmul(ah[...], jnp.concatenate([kh, kl], axis=1))
    signal = both[:, :ch] + both[:, ch:] + matmul(al[...], kh)
    a, b = signal[:length], signal[length:]
    c, e = spectrum[:length], spectrum[length:]
    yh, yl = two_parts(jnp.concatenate([a * c - b * e, a * e + b * c], axis=0))
    for load in loads[3 * n + 2:3 * n + 5]:
        load.wait()
    query[...] = filtered(0)
    y_parts = jnp.concatenate([yh, yl], axis=1)
    send_order = (far_sib, far, sib, t)

    def block_rows(p):
        return pl.ds(pl.multiple_of(p * rows, 128), rows)

    def g_copy(p, to, slot):
        return remote(
            gathered.at[slot, block_rows(p)], gathered.at[slot, block_rows(p)],
            g_send.at[p, to], g_recv.at[p, slot], to, t,
        )

    for p in send_order:
        both = matmul(bh[block_rows(p)], y_parts)
        conv = (both[:, :ch] + both[:, ch:] + matmul(bl[block_rows(p)], yh)) * (1.0 / length)
        gathered[s, block_rows(p)] = (query[block_rows(p)] * conv).astype(jnp.bfloat16)
        for to in others:
            g_copy(p, to, s).start()

    def term(p):
        at = block_rows(p)
        for k in others:
            g_copy(p, k, k).wait_recv()
        return matmul_nt(jnp.concatenate([gathered[i, at] for i in range(n)], axis=1), wo[...])

    def hop(which, target, to_s, to_t, h):
        return remote(
            terms.at[which, piece(h)], target.at[piece(h)], t_send.at[which, h], t_recv.at[which, h], to_s, to_t
        )

    def far_out(h):
        return hop(0, sibling_in.at[0], s, sib, h)

    def own_out(h):
        return hop(1, sibling_in.at[1], s, sib, h)

    def cross(h):
        return hop(2, cross_in, s, far, h)

    def final(h):
        return hop(3, final_in, t, s, h)

    terms[0] = term(far_sib).astype(jnp.bfloat16)
    for h in range(chunks):
        far_out(h).start()
    terms_acc[...] = term(far)
    for h in range(chunks):
        far_out(h).wait_recv()
        terms[2, piece(h)] = (
            terms_acc[piece(h)] + sibling_in[0, piece(h)].astype(jnp.float32)
        ).astype(jnp.bfloat16)
        cross(h).start()
    terms[1] = term(sib).astype(jnp.bfloat16)
    for h in range(chunks):
        own_out(h).start()
    terms_acc[...] = term(t)
    for h in range(chunks):
        own_out(h).wait_recv()
        terms_acc[piece(h)] += sibling_in[1, piece(h)].astype(jnp.float32)
    for h in range(chunks):
        cross(h).wait_recv()
        value = terms_acc[piece(h)] + cross_in[piece(h)].astype(jnp.float32)

        @pl.when(s != t)
        def _():
            terms[3, piece(h)] = value.astype(jnp.bfloat16)
            final(h).start()

        @pl.when(s == t)
        def _():
            out_ref[piece(h)] = x_ref[piece(h)] + value

    @pl.when(s != t)
    def _():
        for h in range(chunks):
            final(h).wait_recv()
            out_ref[piece(h)] = x_ref[piece(h)] + final_in[piece(h)].astype(jnp.float32)
        for h in range(chunks):
            swap(h, s).wait_send()
            final(h).wait_send()

    for h in range(chunks):
        for copy in (
            slot_copy(t, 1, far, h), slot_copy(t, 2, sib, h), slot_copy(far, 3, sib, h),
            far_out(h), own_out(h), cross(h),
        ):
            copy.wait_send()
    for copy in q_copies:
        copy.wait_send()
    for p in order:
        for d in others:
            p_copy(p, d, s).wait_send()

    for p in order:
        for to in others:
            g_copy(p, to, s).wait_send()


def kernel_shards(residual_in, norm_gain, in_weight, short_taps, long_filter, out_weight):
    n = 4
    rows, width = residual_in.shape
    ch, length = long_filter.shape
    tables = [jnp.asarray(table) for table in transform_tables(length)]
    vmem, hbm = pl.BlockSpec(memory_space=pltpu.VMEM), pl.BlockSpec(memory_space=pl.ANY)
    dma = pltpu.SemaphoreType.DMA
    bf16, f32 = jnp.bfloat16, jnp.float32
    return pl.pallas_call(
        block_kernel,
        out_shape=jax.ShapeDtypeStruct((rows, width), f32),
        in_specs=[hbm] * 10,
        out_specs=vmem,
        scratch_shapes=[
            pltpu.VMEM((rows, width), f32),
            pltpu.VMEM((1, width), f32),
            pltpu.VMEM(short_taps.shape[:2] + (ch,), f32),
            pltpu.VMEM((ch, length), f32),
            pltpu.VMEM((n, width, 3 * ch), bf16),
            pltpu.VMEM(out_weight.shape, bf16),
            pltpu.VMEM((2 * length, length), bf16),
            pltpu.VMEM((2 * length, length), bf16),
            pltpu.VMEM((length, 2 * length), bf16),
            pltpu.VMEM((length, 2 * length), bf16),
            pltpu.VMEM((rows, width), bf16),
            pltpu.VMEM((n, rows, width), bf16),
            pltpu.VMEM((n, n, rows, 3 * ch), f32),
            pltpu.VMEM((n, n, rows, 3 * ch), bf16),
            pltpu.VMEM((n, n, rows, 3 * ch), bf16),
            pltpu.VMEM((n, 8, length), f32),
            pltpu.VMEM((2 * length, ch), f32),
            pltpu.VMEM((length, ch), f32),
            pltpu.VMEM((n, length, ch), bf16),
            pltpu.VMEM((n, rows, width), bf16),
            pltpu.VMEM((rows, width), f32),
            pltpu.VMEM((2, rows, width), bf16),
            pltpu.VMEM((rows, width), bf16),
            pltpu.VMEM((rows, width), bf16),
            dma((3 * n + 9,)), dma((n, n)), dma((n, n)), dma((n, n)), dma((n, n)),
            dma((n,)), dma((n,)), dma((n, n)), dma((n, n)), dma((n, n)), dma((n, n)),
        ],
        compiler_params=pltpu.CompilerParams(
            collective_id=0, has_side_effects=True, vmem_limit_bytes=60 * 1024 * 1024
        ),
    )(residual_in, norm_gain[None], in_weight, short_taps, long_filter, out_weight, *tables)


def solution(mesh):
    square = mesh.shape["seq"] == 4 and mesh.shape["tensor"] == 4
    return jax.shard_map(
        kernel_shards if square else shards,
        mesh=mesh,
        in_specs=(
            P(("groups", "seq"), "tensor"),
            P(),
            P(None, "seq", "tensor"),
            P(None, None, "tensor"),
            P(("tensor", "seq"), None),
            P("seq", "tensor"),
        ),
        out_specs=P(("groups", "seq"), "tensor"),
        check_vma=False,
    )
```

```python
import math

import jax
import jax.numpy as jnp
import ml_dtypes
import numpy as np
from jax import lax
from jax.experimental import pallas as pl
from jax.experimental.pallas import tpu as pltpu
from jax.sharding import PartitionSpec as P

EPSILON = 1e-05


def shifted(value, axis, by):
    length = lax.axis_size(axis)
    pairs = [(i, i + by) for i in range(length) if 0 <= i + by < length]
    return lax.ppermute(value, axis, pairs)


def exact_product(form, left, right):
    return jnp.einsum(form, left, right, precision=lax.Precision.HIGHEST)


def angle_tables(modulus, count_a, count_b):
    index_a = jnp.arange(count_a, dtype=jnp.int32)[:, None]
    index_b = jnp.arange(count_b, dtype=jnp.int32)[None, :]
    theta = (index_a * index_b % modulus).astype(jnp.float32) * (2.0 * math.pi / modulus)
    return (jnp.cos(theta), jnp.sin(theta))


def split_length(full_length):
    low_factor = 1
    while full_length % (4 * low_factor) == 0 and 4 * low_factor * low_factor <= full_length:
        low_factor = low_factor * 2
    return (low_factor, full_length // low_factor)


def forward_spectrum(signal, low_factor, high_factor, all_tables):
    cos_high, sin_high, cos_twist, sin_twist, cos_low, sin_low = all_tables
    channel_count = signal.shape[0]
    blocks = signal.reshape(channel_count, high_factor // 2, low_factor)
    real_a = exact_product("cmp,mk->cpk", blocks, cos_high)
    imag_a = -exact_product("cmp,mk->cpk", blocks, sin_high)
    real_b = real_a * cos_twist + imag_a * sin_twist
    imag_b = imag_a * cos_twist - real_a * sin_twist
    real_x = exact_product("cpk,pj->cjk", real_b, cos_low) + exact_product(
        "cpk,pj->cjk", imag_b, sin_low
    )
    imag_x = exact_product("cpk,pj->cjk", imag_b, cos_low) - exact_product(
        "cpk,pj->cjk", real_b, sin_low
    )
    return (real_x, imag_x)


def inverse_signal(real_x, imag_x, low_factor, high_factor, all_tables):
    cos_high, sin_high, cos_twist, sin_twist, cos_low, sin_low = all_tables
    channel_count = real_x.shape[0]
    real_b = exact_product("cjk,pj->cpk", real_x, cos_low) - exact_product(
        "cjk,pj->cpk", imag_x, sin_low
    )
    imag_b = exact_product("cjk,pj->cpk", real_x, sin_low) + exact_product(
        "cjk,pj->cpk", imag_x, cos_low
    )
    real_c = real_b * cos_twist - imag_b * sin_twist
    imag_c = real_b * sin_twist + imag_b * cos_twist
    result = exact_product("cpk,mk->cmp", real_c, cos_high) - exact_product(
        "cpk,mk->cmp", imag_c, sin_high
    )
    full_length = low_factor * high_factor
    return (result / full_length).reshape(channel_count, full_length // 2)


def shards(residual_in, norm_gain, in_weight, short_taps, long_filter, out_weight):
    row_count, local_width = residual_in.shape
    full_rows = lax.all_gather(
        residual_in.astype(jnp.bfloat16), "tensor", axis=1, tiled=True
    ).astype(residual_in.dtype)
    mean_sq = jnp.mean(full_rows * full_rows, axis=1, keepdims=True)
    normed = (full_rows * lax.rsqrt(mean_sq + EPSILON) * norm_gain).astype(jnp.bfloat16)
    projected = jnp.einsum(
        "rd,sdc->scr",
        normed,
        lax.all_gather(in_weight, "seq", axis=1, tiled=True),
        preferred_element_type=jnp.float32,
    )
    reach = short_taps.shape[1] - 1
    earlier = shifted(projected[:, :, row_count - reach :], "seq", 1)
    extended = jnp.concatenate([earlier, projected], axis=2)
    mixed = short_taps[:, 0, :, None] * projected
    for offset in range(1, reach + 1):
        mixed = (
            mixed
            + short_taps[:, offset, :, None]
            * extended[:, :, reach - offset : reach - offset + row_count]
        )
    query = mixed[0]
    product_kv = mixed[1] * mixed[2]
    by_channel = lax.all_to_all(
        product_kv.astype(jnp.bfloat16), "seq", split_axis=0, concat_axis=1, tiled=True
    ).astype(product_kv.dtype)
    full_length = 2 * by_channel.shape[1]
    low_factor, high_factor = split_length(full_length)
    cos_high, sin_high = angle_tables(high_factor, high_factor // 2, high_factor)
    cos_twist, sin_twist = angle_tables(full_length, low_factor, high_factor)
    cos_low, sin_low = angle_tables(low_factor, low_factor, low_factor)
    all_tables = (cos_high, sin_high, cos_twist, sin_twist, cos_low, sin_low)
    signal_real, signal_imag = forward_spectrum(by_channel, low_factor, high_factor, all_tables)
    filter_real, filter_imag = forward_spectrum(long_filter, low_factor, high_factor, all_tables)
    conv = inverse_signal(
        signal_real * filter_real - signal_imag * filter_imag,
        signal_real * filter_imag + signal_imag * filter_real,
        low_factor,
        high_factor,
        all_tables,
    )
    returned = lax.all_to_all(
        conv.astype(jnp.bfloat16), "seq", split_axis=1, concat_axis=0, tiled=True
    ).astype(conv.dtype)
    gated = (query * returned).astype(jnp.bfloat16)
    terms = jnp.einsum(
        "cr,nc->rn",
        gated,
        lax.all_gather(out_weight, "seq", axis=0, tiled=True),
        preferred_element_type=jnp.float32,
    )
    summed = lax.psum_scatter(
        terms.astype(jnp.bfloat16), "tensor", scatter_dimension=1, tiled=True
    ).astype(jnp.float32)
    return residual_in + summed


MESH = pl.DeviceIdType.MESH


def transform_tables(length):
    index = np.arange(length)
    turns = ((2 * index[:, None] + 1) * index[None, :]) % (4 * length)
    theta = turns.astype(np.float64) * (math.pi / (2 * length))
    table = np.concatenate([np.cos(theta), np.sin(theta)], axis=0).astype(np.float32)
    high = table.astype(ml_dtypes.bfloat16)
    low = (table - high.astype(np.float32)).astype(ml_dtypes.bfloat16)
    return (high, low, np.ascontiguousarray(high.T), np.ascontiguousarray(low.T))


def two_parts(value):
    high = value.astype(jnp.bfloat16)
    low = (value - high.astype(jnp.float32)).astype(jnp.bfloat16)
    return (high, low)


def matmul(left, right):
    return jnp.dot(left, right, preferred_element_type=jnp.float32)


def matmul_nt(left, right):
    return lax.dot_general(left, right, (((1,), (1,)), ((), ())), preferred_element_type=jnp.float32)


def block_kernel(
    x_hbm, gain_hbm, w_hbm, taps_hbm, filter_hbm, wo_hbm, ah_hbm, al_hbm, bh_hbm, bl_hbm,
    out_ref,
    x_ref, gain_ref, taps_ref, filter_ref, wv, wo, ah, al, bh, bl, xb, xg, part, send_kv, send_q, inbox_kv, inbox_q, squares, spectrum,
    gathered, terms, terms_acc, sibling_in, cross_in, final_in,
    load_sem, x_send, x_recv, p_send, p_recv, q_send, q_recv,
    g_right, g_left, g_recv, t_send, t_recv,
):
    s = lax.axis_index("seq")
    t = lax.axis_index("tensor")
    n = 4
    rows, width = x_ref.shape
    ch = filter_ref.shape[0]
    length = filter_ref.shape[1]
    sib = t + 1 - 2 * lax.rem(t, 2)
    far = lax.rem(t + 2, n)
    far_sib = lax.rem(sib + 2, n)

    chunks = 4
    step = rows // chunks

    def lanes(i):
        return pl.ds(pl.multiple_of(i * ch, 128), ch)

    loads = []
    for d in range(n):
        for j in range(3):
            loads.append(pltpu.make_async_copy(
                w_hbm.at[(j + 1) % 3, :, pl.ds(d * ch, ch)],
                wv.at[d, :, pl.ds(j * ch, ch)],
                load_sem.at[d * 3 + j],
            ))
    for i, (source, target) in enumerate((
        (ah_hbm, ah), (al_hbm, al), (wo_hbm, wo), (bh_hbm, bh), (bl_hbm, bl),
        (x_hbm, x_ref), (filter_hbm, filter_ref), (taps_hbm.at[:, :, lanes(s)], taps_ref),
        (gain_hbm.at[:, pl.ds(pl.multiple_of(s * width, 128), width)], gain_ref),
    )):
        loads.append(pltpu.make_async_copy(source, target, load_sem.at[3 * n + i]))
    x_load, filter_load, taps_load, gain_load = loads[3 * n + 5:]
    x_load.start()

    barrier = pltpu.get_barrier_semaphore()
    for k in range(1, n):
        pl.semaphore_signal(barrier, inc=1, device_id={"seq": lax.rem(s + k, n), "tensor": t}, device_id_type=MESH)
        pl.semaphore_signal(barrier, inc=1, device_id={"seq": s, "tensor": lax.rem(t + k, n)}, device_id_type=MESH)

    @pl.when(s != t)
    def _():
        pl.semaphore_signal(barrier, inc=1, device_id={"seq": t, "tensor": s}, device_id_type=MESH)

    x_load.wait()
    xb[...] = x_ref[...].astype(jnp.bfloat16)

    @pl.when(s != t)
    def _():
        pl.semaphore_wait(barrier, 2 * n - 1)

    @pl.when(s == t)
    def _():
        pl.semaphore_wait(barrier, 2 * n - 2)

    def remote(source, target, send, recv, to_s, to_t):
        return pltpu.make_async_remote_copy(
            src_ref=source, dst_ref=target, send_sem=send, recv_sem=recv,
            device_id={"seq": to_s, "tensor": to_t}, device_id_type=MESH,
        )

    def piece(h):
        return pl.ds(h * step, step)

    def swap(h, slot):
        return remote(
            xb.at[piece(h)], xg.at[slot, piece(h)], x_send.at[0, h], x_recv.at[slot, h], t, s
        )

    @pl.when(s != t)
    def _():
        for h in range(chunks):
            swap(h, s).start()

    gain_load.start()
    for load in loads[:3 * n] + [filter_load] + loads[3 * n:3 * n + 2] + [taps_load] + loads[3 * n + 2:3 * n + 5]:
        load.start()

    def slot_copy(slot, which, to_t, h):
        return remote(
            xg.at[slot, piece(h)], xg.at[slot, piece(h)], x_send.at[which, h], x_recv.at[slot, h], s, to_t
        )

    @pl.when(s == t)
    def _():
        xg[t] = xb[...]

    for h in range(chunks):
        @pl.when(s != t)
        def _():
            swap(h, t).wait_recv()

        slot_copy(t, 1, far, h).start()
        slot_copy(t, 2, sib, h).start()

    for load in loads[: 3 * n]:
        load.wait()
    gain_load.wait()
    gain = gain_ref[...]
    ones = jnp.ones((8, width), jnp.bfloat16)

    cuts = (slice(0, 2 * ch), slice(2 * ch, 3 * ch))
    sendb, inbox = (send_kv, send_q), (inbox_kv, inbox_q)

    def p_copy(p, d, slot, q):
        return remote(
            sendb[q].at[p, d], inbox[q].at[p, slot], p_send.at[q, p, d], p_recv.at[q, p, slot], d, t
        )

    others = [lax.rem(s + k, n) for k in (2, 1, 3)]

    def dots(p):
        features = xg[p].astype(jnp.float32)
        sh, sl = two_parts(features * features)
        squares[s, :, pl.ds(pl.multiple_of(p * rows, 128), rows)] = matmul_nt(ones, sh) + matmul_nt(ones, sl)
        y = (features * gain).astype(jnp.bfloat16)

        @pl.loop(0, n)
        def _(d):
            part[p, d] = matmul(y, wv[d])

        for d in others:
            sendb[0][p, d] = part[p, d, :, cuts[0]].astype(jnp.bfloat16)
            p_copy(p, d, s, 0).start()
            sendb[1][p, d] = part[p, d, :, cuts[1]].astype(jnp.bfloat16)

    def total(p, q):
        for k in others:
            p_copy(p, k, k, q).wait_recv()
        value = part[p, s, :, cuts[q]]
        for k in others:
            value = value + inbox[q][p, k].astype(jnp.float32)
        part[p, s, :, cuts[q]] = value

    order = (t, sib, far, far_sib)
    dots(t)
    for h in range(chunks):
        slot_copy(far, 1, far, h).wait_recv()
        slot_copy(far, 3, sib, h).start()
    for h in range(chunks):
        slot_copy(sib, 2, sib, h).wait_recv()
    dots(sib)
    dots(far)
    for h in range(chunks):
        slot_copy(far_sib, 3, sib, h).wait_recv()
    dots(far_sib)

    q_copies = []
    for k in range(1, n):
        q_copy = remote(squares.at[s], squares.at[s], q_send.at[k], q_recv.at[s], lax.rem(s + k, n), t)
        q_copy.start()
        q_copies.append(q_copy)
    filter_load.wait()
    fh, fl = two_parts(filter_ref[...])
    loads[3 * n].wait()
    loads[3 * n + 1].wait()
    spectrum[...] = matmul_nt(ah[...], fh) + matmul_nt(ah[...], fl) + matmul_nt(al[...], fh)


    for k in range(1, n):
        other = lax.rem(s + k, n)
        remote(squares.at[other], squares.at[other], q_send.at[k], q_recv.at[other], other, t).wait_recv()
    all_squares = squares[0] + squares[1] + squares[2] + squares[3]
    scale = lax.rsqrt(all_squares * (1.0 / (n * width)) + EPSILON)
    scale = jnp.transpose(jnp.broadcast_to(scale[0:1], (ch, length)))
    taps_load.wait()
    for p in order:
        for d in others:
            p_copy(p, d, s, 0).wait_send()
    for p in order:
        for d in others:
            p_copy(p, d, s, 1).start()
    for p in order:
        total(p, 0)

    row = lax.broadcasted_iota(jnp.int32, (length, ch), 0)

    def filtered(j):
        at = (j + 2) % 3 * ch
        projected = jnp.concatenate([part[p, s, :, at:at + ch] for p in range(n)], axis=0) * scale
        taps = [taps_ref[j, o:o + 1, :] for o in range(3)]
        value = taps[0] * projected
        for o in range(1, 3):
            value = value + taps[o] * jnp.where(row >= o, pltpu.roll(projected, o, 0), 0.0)
        return value

    kh, kl = two_parts(filtered(1) * filtered(2))
    both = matmul(ah[...], jnp.concatenate([kh, kl], axis=1))
    signal = both[:, :ch] + both[:, ch:] + matmul(al[...], kh)
    a, b = signal[:length], signal[length:]
    c, e = spectrum[:length], spectrum[length:]
    yh, yl = two_parts(jnp.concatenate([a * c - b * e, a * e + b * c], axis=0))
    for load in loads[3 * n + 2:3 * n + 5]:
        load.wait()
    both = matmul(bh[...], jnp.concatenate([yh, yl], axis=1))
    conv = (both[:, :ch] + both[:, ch:] + matmul(bl[...], yh)) * (1.0 / length)
    for p in order:
        total(p, 1)
    query = filtered(0)

    gathered[s] = (query * conv).astype(jnp.bfloat16)

    def g_copy(i, up):
        sems = g_right if up else g_left
        return remote(
            gathered.at[i], gathered.at[i], sems.at[i], g_recv.at[i],
            s + 1 if up else s - 1, t,
        )

    @pl.when(s < n - 1)
    def _():
        g_copy(s, True).start()

    @pl.when(s > 0)
    def _():
        g_copy(s, False).start()

    for k in range(1, n):
        @pl.when(s - k >= 0)
        def _():
            g_copy(s - k, True).wait_recv()

            @pl.when(s < n - 1)
            def _():
                g_copy(s - k, True).start()

        @pl.when(s + k < n)
        def _():
            g_copy(s + k, False).wait_recv()

            @pl.when(s > 0)
            def _():
                g_copy(s + k, False).start()

    def term(p):
        at = pl.ds(pl.multiple_of(p * rows, 128), rows)
        return matmul_nt(jnp.concatenate([gathered[i, at] for i in range(n)], axis=1), wo[...])

    def hop(which, target, to_s, to_t, h):
        return remote(
            terms.at[which, piece(h)], target.at[piece(h)], t_send.at[which, h], t_recv.at[which, h], to_s, to_t
        )

    def far_out(h):
        return hop(0, sibling_in.at[0], s, sib, h)

    def own_out(h):
        return hop(1, sibling_in.at[1], s, sib, h)

    def cross(h):
        return hop(2, cross_in, s, far, h)

    def final(h):
        return hop(3, final_in, t, s, h)

    terms[0] = term(far_sib).astype(jnp.bfloat16)
    for h in range(chunks):
        far_out(h).start()
    terms_acc[...] = term(far)
    for h in range(chunks):
        far_out(h).wait_recv()
        terms[2, piece(h)] = (
            terms_acc[piece(h)] + sibling_in[0, piece(h)].astype(jnp.float32)
        ).astype(jnp.bfloat16)
        cross(h).start()
    terms[1] = term(sib).astype(jnp.bfloat16)
    for h in range(chunks):
        own_out(h).start()
    terms_acc[...] = term(t)
    for h in range(chunks):
        own_out(h).wait_recv()
        terms_acc[piece(h)] += sibling_in[1, piece(h)].astype(jnp.float32)
    for h in range(chunks):
        cross(h).wait_recv()
        value = terms_acc[piece(h)] + cross_in[piece(h)].astype(jnp.float32)

        @pl.when(s != t)
        def _():
            terms[3, piece(h)] = value.astype(jnp.bfloat16)
            final(h).start()

        @pl.when(s == t)
        def _():
            out_ref[piece(h)] = x_ref[piece(h)] + value

    @pl.when(s != t)
    def _():
        for h in range(chunks):
            final(h).wait_recv()
            out_ref[piece(h)] = x_ref[piece(h)] + final_in[piece(h)].astype(jnp.float32)
        for h in range(chunks):
            swap(h, s).wait_send()
            final(h).wait_send()

    for h in range(chunks):
        for copy in (
            slot_copy(t, 1, far, h), slot_copy(t, 2, sib, h), slot_copy(far, 3, sib, h),
            far_out(h), own_out(h), cross(h),
        ):
            copy.wait_send()
    for copy in q_copies:
        copy.wait_send()
    for p in order:
        for d in others:
            p_copy(p, d, s, 1).wait_send()

    @pl.loop(0, n)
    def _(i):
        @pl.when((i <= s) & (s < n - 1))
        def _():
            g_copy(i, True).wait_send()

        @pl.when((i >= s) & (s > 0))
        def _():
            g_copy(i, False).wait_send()


def kernel_shards(residual_in, norm_gain, in_weight, short_taps, long_filter, out_weight):
    n = 4
    rows, width = residual_in.shape
    ch, length = long_filter.shape
    tables = [jnp.asarray(table) for table in transform_tables(length)]
    vmem, hbm = pl.BlockSpec(memory_space=pltpu.VMEM), pl.BlockSpec(memory_space=pl.ANY)
    dma = pltpu.SemaphoreType.DMA
    bf16, f32 = jnp.bfloat16, jnp.float32
    return pl.pallas_call(
        block_kernel,
        out_shape=jax.ShapeDtypeStruct((rows, width), f32),
        in_specs=[hbm] * 10,
        out_specs=vmem,
        scratch_shapes=[
            pltpu.VMEM((rows, width), f32),
            pltpu.VMEM((1, width), f32),
            pltpu.VMEM(short_taps.shape[:2] + (ch,), f32),
            pltpu.VMEM((ch, length), f32),
            pltpu.VMEM((n, width, 3 * ch), bf16),
            pltpu.VMEM(out_weight.shape, bf16),
            pltpu.VMEM((2 * length, length), bf16),
            pltpu.VMEM((2 * length, length), bf16),
            pltpu.VMEM((length, 2 * length), bf16),
            pltpu.VMEM((length, 2 * length), bf16),
            pltpu.VMEM((rows, width), bf16),
            pltpu.VMEM((n, rows, width), bf16),
            pltpu.VMEM((n, n, rows, 3 * ch), f32),
            pltpu.VMEM((n, n, rows, 2 * ch), bf16),
            pltpu.VMEM((n, n, rows, ch), bf16),
            pltpu.VMEM((n, n, rows, 2 * ch), bf16),
            pltpu.VMEM((n, n, rows, ch), bf16),
            pltpu.VMEM((n, 8, length), f32),
            pltpu.VMEM((2 * length, ch), f32),
            pltpu.VMEM((n, length, ch), bf16),
            pltpu.VMEM((n, rows, width), bf16),
            pltpu.VMEM((rows, width), f32),
            pltpu.VMEM((2, rows, width), bf16),
            pltpu.VMEM((rows, width), bf16),
            pltpu.VMEM((rows, width), bf16),
            dma((3 * n + 9,)), dma((n, n)), dma((n, n)), dma((2, n, n)), dma((2, n, n)),
            dma((n,)), dma((n,)), dma((n,)), dma((n,)), dma((n,)), dma((n, n)), dma((n, n)),
        ],
        compiler_params=pltpu.CompilerParams(
            collective_id=0, has_side_effects=True, vmem_limit_bytes=60 * 1024 * 1024
        ),
    )(residual_in, norm_gain[None], in_weight, short_taps, long_filter, out_weight, *tables)


def solution(mesh):
    square = mesh.shape["seq"] == 4 and mesh.shape["tensor"] == 4
    return jax.shard_map(
        kernel_shards if square else shards,
        mesh=mesh,
        in_specs=(
            P(("groups", "seq"), "tensor"),
            P(),
            P(None, "seq", "tensor"),
            P(None, None, "tensor"),
            P(("tensor", "seq"), None),
            P("seq", "tensor"),
        ),
        out_specs=P(("groups", "seq"), "tensor"),
        check_vma=False,
    )
```
